128 devices in a mesh: scan: 4 (over z_lo, core), pts: 32 (over y, x, z_hi).
Axes of the slice: x: 4, y: 4, z: 4 (z_hi: 2, z_lo: 2; z = z_hi * 2 + z_lo), core: 2. Of those that a mesh axis runs over, the one named last changes fastest.
Arguments:
- cotangent: bfloat16 [2048, 131072], P('scan', 'pts'), may hold values from -6 to 6
- scan_paths: bfloat16 [2048, 256], P('scan'), may hold values from -6 to 6
- query_points: bfloat16 [4, 131072], P(None, 'pts'), may hold values from -1 to 1
- branch_in: bfloat16 [256, 2048], replicated, may hold values from -0.375 to 0.375
- branch_in_bias: float32 [2048], replicated, may hold values from -3 to 3
- branch_out: bfloat16 [2048, 512], replicated, may hold values from -0.125 to 0.125
- branch_out_bias: float32 [512], replicated, may hold values from -3 to 3
- trunk_in: bfloat16 [4, 1024], replicated, may hold values from -6 to 6
- trunk_in_bias: float32 [1024], replicated, may hold values from -4.5 to 4.5
- trunk_mid: bfloat16 [1, 1024, 1024], replicated, may hold values from -0.1875 to 0.1875
- trunk_mid_bias: float32 [1, 1024], replicated, may hold values from -3 to 3
- trunk_out: bfloat16 [1024, 512], replicated, may hold values from -0.1875 to 0.1875
- trunk_out_bias: float32 [512], replicated, may hold values from -3 to 3
Outputs:
- grad_branch_in: float32 [256, 2048], replicated
- grad_branch_in_bias: float32 [2048], replicated
- grad_branch_out: float32 [2048, 512], replicated
- grad_branch_out_bias: float32 [512], replicated
- grad_trunk_in: float32 [4, 1024], replicated
- grad_trunk_in_bias: float32 [1024], replicated
- grad_trunk_mid: float32 [1, 1024, 1024], replicated
- grad_trunk_mid_bias: float32 [1, 1024], replicated
- grad_trunk_out: float32 [1024, 512], replicated
- grad_trunk_out_bias: float32 [512], replicated
The draws below stay inside these ranges and needn't reach their ends.
All inputs are finite; a program needn't handle non-finite values.
Results may differ from the reference program's by a relative error of at most 0.012.
Values may be sent and summed in bfloat16 or wider, within the bound.
No kernel may reach another device: no remote copies, remote signals or barrier semaphores. Data moves between devices by JAX's collectives and lax.ppermute only.
A program may use at most 128 MiB of HBM per device.

```python
import math
import jax
import jax.numpy as jnp
from jax import lax

SAMPLES = 256
BRANCH_W = 2048
BASIS = 512
TRUNK_W = 1024
COORDS = 4
MID_LAYERS = 1
SCANS = 2048
POINTS = 131072


def block_scale(key, dims, shards, low, top_value):
    def one(axis_at, shards_of):
        steps = jax.random.uniform(jax.random.fold_in(jax.random.fold_in(key, 6), axis_at), (shards_of,), jnp.float32, low / len(shards), top_value / len(shards))
        return jnp.repeat(jnp.exp(steps), dims[axis_at] // shards_of).reshape((-1,) + (1,) * (len(dims) - axis_at - 1))

    factor_of = one(*shards[0])
    for cut in shards[1:]:
        factor_of = factor_of * one(*cut)
    return factor_of


def gaussian(stream_key, extent, deviation, most, cuts=(), kind=jnp.bfloat16):
    values = jax.random.normal(stream_key, extent, jnp.float32) * deviation
    if len(cuts) > 0:
        values = block_scale(stream_key, extent, cuts, -0.22, 0.18) * values
    return jnp.clip(values, min=-most, max=most).astype(kind)


def setup_inputs(seed: int = 0) -> dict:
    arg_keys = jax.random.split(jax.random.key(seed), 14)
    cotangent = gaussian(arg_keys[0], (SCANS, POINTS), 1.0, 6.0, ((0, 4), (1, 32)))
    scan_paths = gaussian(arg_keys[1], (SCANS, SAMPLES), 1.0, 6.0, ((0, 4),))
    query_points = jnp.clip(jax.random.uniform(arg_keys[2], (COORDS, POINTS), jnp.float32, -1.0, 1.0) * block_scale(arg_keys[2], (COORDS, POINTS), ((1, 32),), -0.4, 0.0), -1.0, 1.0).astype(jnp.bfloat16)
    branch_in = gaussian(arg_keys[3], (SAMPLES, BRANCH_W), SAMPLES ** -0.5, 0.375)
    branch_in_bias = gaussian(arg_keys[4], (BRANCH_W,), 0.5, 3.0, (), jnp.float32)
    branch_out = gaussian(arg_keys[5], (BRANCH_W, BASIS), BRANCH_W ** -0.5, 0.125)
    branch_out_bias = gaussian(arg_keys[6], (BASIS,), 0.5, 3.0, (), jnp.float32)
    trunk_in = gaussian(arg_keys[7], (COORDS, TRUNK_W), 2.0, 6.0)
    trunk_in_bias = gaussian(arg_keys[8], (TRUNK_W,), 1.5, 4.5, (), jnp.float32)
    trunk_mid = gaussian(arg_keys[9], (MID_LAYERS, TRUNK_W, TRUNK_W), TRUNK_W ** -0.5, 0.1875)
    trunk_mid_bias = gaussian(arg_keys[10], (MID_LAYERS, TRUNK_W), 0.5, 3.0, (), jnp.float32)
    trunk_out = gaussian(arg_keys[11], (TRUNK_W, BASIS), TRUNK_W ** -0.5, 0.1875)
    trunk_out_bias = gaussian(arg_keys[12], (BASIS,), 0.5, 3.0, (), jnp.float32)
    return {"cotangent": cotangent, "scan_paths": scan_paths, "query_points": query_points, "branch_in": branch_in, "branch_in_bias": branch_in_bias, "branch_out": branch_out, "branch_out_bias": branch_out_bias, "trunk_in": trunk_in, "trunk_in_bias": trunk_in_bias, "trunk_mid": trunk_mid, "trunk_mid_bias": trunk_mid_bias, "trunk_out": trunk_out, "trunk_out_bias": trunk_out_bias}


def tanh_layer(inputs, weights, offsets):
    summed = jnp.dot(inputs, weights, preferred_element_type=jnp.float32) + offsets
    return jnp.tanh(summed).astype(jnp.bfloat16)

def back_layer(upstream, weights, outputs):
    pulled = jnp.dot(upstream, weights.T, preferred_element_type=jnp.float32)
    values = outputs.astype(jnp.float32)
    return (pulled * (1.0 - values * values)).astype(jnp.bfloat16)

def column_sums(values):
    return lax.optimization_barrier(jnp.sum(values.astype(jnp.float32), axis=0))

def reference(cotangent, scan_paths, query_points, branch_in, branch_in_bias, branch_out, branch_out_bias, trunk_in, trunk_in_bias, trunk_mid, trunk_mid_bias, trunk_out, trunk_out_bias):
    hidden_branch = tanh_layer(scan_paths, branch_in, branch_in_bias)
    coeffs = (jnp.dot(hidden_branch, branch_out, preferred_element_type=jnp.float32) + branch_out_bias).astype(jnp.bfloat16)
    layers = [tanh_layer(query_points.T, trunk_in, trunk_in_bias)]
    for layer_idx in range(MID_LAYERS):
        layers.append(tanh_layer(layers[-1], trunk_mid[layer_idx], trunk_mid_bias[layer_idx]))
    basis_vals = tanh_layer(layers[-1], trunk_out, trunk_out_bias)
    factor = 1.0 / math.sqrt(SCANS * POINTS)
    coef_grad = factor * jnp.dot(cotangent, basis_vals, preferred_element_type=jnp.float32)
    coef_low = coef_grad.astype(jnp.bfloat16)
    basis_grad = factor * jnp.dot(cotangent.T, coeffs, preferred_element_type=jnp.float32)
    basis_wide = basis_vals.astype(jnp.float32)
    deltas = (basis_grad * (1.0 - basis_wide * basis_wide)).astype(jnp.bfloat16)
    grad_trunk_out = jnp.dot(layers[-1].T, deltas, preferred_element_type=jnp.float32)
    grad_trunk_out_bias = column_sums(deltas)
    mid_grads = [None] * MID_LAYERS
    mid_biases = [None] * MID_LAYERS
    weights_next = trunk_out
    for layer_idx in range(MID_LAYERS, 0, -1):
        deltas = back_layer(deltas, weights_next, layers[layer_idx])
        mid_grads[layer_idx - 1] = jnp.dot(layers[layer_idx - 1].T, deltas, preferred_element_type=jnp.float32)
        mid_biases[layer_idx - 1] = column_sums(deltas)
        weights_next = trunk_mid[layer_idx - 1]
    deltas = back_layer(deltas, weights_next, layers[0])
    grad_trunk_in = jnp.dot(query_points, deltas, preferred_element_type=jnp.float32)
    grad_trunk_in_bias = column_sums(deltas)
    grad_trunk_mid = jnp.stack(mid_grads)
    grad_trunk_mid_bias = jnp.stack(mid_biases)
    grad_branch_out = jnp.dot(hidden_branch.T, coef_low, preferred_element_type=jnp.float32)
    grad_branch_out_bias = lax.optimization_barrier(jnp.sum(coef_grad, axis=0))
    branch_delta = back_layer(coef_low, branch_out, hidden_branch)
    grad_branch_in = jnp.dot(scan_paths.T, branch_delta, preferred_element_type=jnp.float32)
    grad_branch_in_bias = column_sums(branch_delta)
    return (grad_branch_in, grad_branch_in_bias, grad_branch_out, grad_branch_out_bias, grad_trunk_in, grad_trunk_in_bias, grad_trunk_mid, grad_trunk_mid_bias, grad_trunk_out, grad_trunk_out_bias)
```

```python
import math

import jax
import jax.numpy as jnp
from jax import lax
from jax.sharding import Mesh, PartitionSpec as P

ALL = ("zl", "core", "y", "x", "zh")
CHIPS = ("zl", "y", "x", "zh")
PTS = ("y", "x", "zh")
BF = jnp.bfloat16
F32 = jnp.float32


def dot(left, right, dims):
    return lax.dot_general(left, right, (dims, ((), ())), preferred_element_type=F32)


def rows_rows(left, right):
    return dot(left, right, ((0,), (0,)))


def swap(values, axis):
    return lax.ppermute(values, axis, [(0, 1), (1, 0)])


def exchange(values, axes):
    return lax.all_to_all(values, axes, split_axis=0, concat_axis=0, tiled=True)


def sum_parts(values):
    return jnp.sum(values.astype(F32), axis=0)


def tanh_layer(inputs, weights, offsets):
    return jnp.tanh(dot(inputs, weights, ((1,), (0,))) + offsets).astype(BF)


def slope(values):
    wide = values.astype(F32)
    return 1.0 - wide * wide


def on_device(
    cotangent,
    scan_paths,
    query_points,
    branch_in,
    branch_in_bias,
    branch_out,
    branch_out_bias,
    trunk_in,
    trunk_in_bias,
    trunk_mid,
    trunk_mid_bias,
    trunk_out,
    trunk_out_bias,
):
    core = lax.axis_index("core")
    scan_rows, point_cols = cotangent.shape
    half = point_cols // 2
    chips = lax.axis_size(CHIPS)
    pts = lax.axis_size(PTS)
    factor = 1.0 / math.sqrt(scan_rows * 4 * point_cols * pts)
    width = trunk_in.shape[1]
    basis = trunk_out.shape[1]

    sent = lax.dynamic_slice_in_dim(cotangent, (1 - core) * half, half, 1)
    kept = lax.dynamic_slice_in_dim(cotangent, core * half, half, 1)
    theirs = swap(sent, "core")
    points = lax.dynamic_slice_in_dim(query_points, core * half, half, 1)

    pair_paths = swap(scan_paths, "core")
    side_paths = swap(jnp.stack([scan_paths, pair_paths]), "zl")

    trunk_0 = jnp.tanh(rows_rows(points, trunk_in) + trunk_in_bias).astype(BF)
    trunk_1 = tanh_layer(trunk_0, trunk_mid[0], trunk_mid_bias[0])
    basis_vals = tanh_layer(trunk_1, trunk_out, trunk_out_bias)

    coef_theirs = dot(theirs, basis_vals, ((1,), (0,))).astype(BF)
    coef_mine = dot(kept, basis_vals, ((1,), (0,)))
    coef_part = (coef_mine + swap(coef_theirs, "core").astype(F32)).astype(BF)
    coef_parts = exchange(coef_part.reshape(pts, scan_rows // pts, basis), PTS)
    coef_low = (factor * sum_parts(coef_parts)).astype(BF)

    hidden_mine = tanh_layer(scan_paths, branch_in, branch_in_bias)
    coeffs = (dot(hidden_mine, branch_out, ((1,), (0,))) + branch_out_bias).astype(BF)
    coeffs_theirs = swap(coeffs, "core")

    basis_grad = factor * (rows_rows(kept, coeffs) + rows_rows(theirs, coeffs_theirs))
    delta_2 = (basis_grad * slope(basis_vals)).astype(BF)
    grad_out = rows_rows(trunk_1, delta_2)
    delta_1 = (dot(delta_2, trunk_out, ((1,), (1,))) * slope(trunk_1)).astype(BF)
    grad_mid = rows_rows(trunk_0, delta_1)
    delta_0 = (dot(delta_1, trunk_mid[0], ((1,), (1,))) * slope(trunk_0)).astype(BF)
    grad_in = dot(points, delta_0, ((1,), (0,)))
    bias_0 = jnp.sum(delta_0.astype(F32), axis=0)
    bias_1 = jnp.sum(delta_1.astype(F32), axis=0)
    bias_2 = jnp.sum(delta_2.astype(F32), axis=0)
    small = jnp.concatenate(
        [grad_in, bias_0[None], bias_1[None], jnp.pad(bias_2, (0, width - basis))[None]], axis=0
    )
    small = jnp.pad(small.T, ((0, 0), (0, 128 - small.shape[0])))
    packed = jnp.concatenate([grad_mid, grad_out, small], axis=1)

    upper, lower = packed[: width // 2], packed[width // 2 :]
    mine = jnp.where(core == 0, upper, lower)
    other = jnp.where(core == 0, lower, upper).astype(BF)
    pair = (mine + swap(other, "core").astype(F32)).astype(BF)
    columns = pair.shape[1]
    rows = width // 2 // chips
    coef_flat = coef_low.reshape(rows, -1)
    load = jnp.concatenate(
        [
            pair.reshape(chips, rows, columns),
            jnp.broadcast_to(coef_flat[None], (chips,) + coef_flat.shape),
        ],
        axis=2,
    )
    got = exchange(load, CHIPS)
    total = sum_parts(got[:, :, :columns]).astype(BF)
    spread = exchange(jnp.broadcast_to(total[None], (chips, rows, columns)), CHIPS)
    spread = spread.reshape(width // 2, columns)
    spread_theirs = swap(spread, "core")

    coef_own = got[:, :, columns:].reshape(2, scan_rows, basis)
    coef_other = swap(coef_own, "core")
    zl = lax.axis_index("zl")
    local_paths = jnp.stack([scan_paths, pair_paths])
    paths = jnp.where(
        zl == 0,
        jnp.stack([local_paths, side_paths], axis=1),
        jnp.stack([side_paths, local_paths], axis=1),
    ).reshape(4 * scan_rows, -1)
    coef_all = jnp.stack([coef_own, coef_other]).reshape(4 * scan_rows, basis)
    hidden = tanh_layer(paths, branch_in, branch_in_bias)
    grad_branch_out = rows_rows(hidden, coef_all)
    grad_branch_out_bias = jnp.sum(coef_all.astype(F32), axis=0)
    branch_delta = (dot(coef_all, branch_out, ((1,), (1,))) * slope(hidden)).astype(BF)
    grad_branch_in = rows_rows(paths, branch_delta)
    grad_branch_in_bias = jnp.sum(branch_delta.astype(F32), axis=0)

    full = jnp.where(
        core == 0,
        jnp.concatenate([spread, spread_theirs], axis=0),
        jnp.concatenate([spread_theirs, spread], axis=0),
    ).astype(F32)
    tail = full[:, width + basis :]
    return (
        grad_branch_in,
        grad_branch_in_bias,
        grad_branch_out,
        grad_branch_out_bias,
        tail[:, :4].T,
        tail[:, 4],
        full[:, :width][None],
        tail[:, 5][None],
        full[:, width : width + basis],
        tail[:basis, 6],
    )


def solution(mesh):
    fine = Mesh(mesh.devices.reshape(2, 2, 4, 4, 2), ALL)
    scan, pts = ("zl", "core"), PTS
    placed = (P(scan, pts), P(scan, None), P(None, pts)) + (P(),) * 10
    return jax.shard_map(
        on_device, mesh=fine, in_specs=placed, out_specs=(P(),) * 10, check_vma=False
    )
```

```python
import functools
import math

import jax
import jax.numpy as jnp
from jax import lax
from jax.experimental import pallas as pl
from jax.experimental.pallas import tpu as pltpu
from jax.sharding import Mesh, PartitionSpec as P

ALL = ("zl", "core", "y", "x", "zh")
CHIPS = ("zl", "y", "x", "zh")
PTS = ("y", "x", "zh")
BF = jnp.bfloat16
F32 = jnp.float32


def dot(left, right, dims):
    return lax.dot_general(left, right, (dims, ((), ())), preferred_element_type=F32)


def rows_rows(left, right):
    return dot(left, right, ((0,), (0,)))


def swap(values, axis):
    return lax.ppermute(values, axis, [(0, 1), (1, 0)])


def exchange(values, axes):
    return lax.all_to_all(values, axes, split_axis=0, concat_axis=0, tiled=True)


def sum_parts(values):
    return jnp.sum(values.astype(F32), axis=0)


def tanh_layer(inputs, weights, offsets):
    return jnp.tanh(dot(inputs, weights, ((1,), (0,))) + offsets).astype(BF)


def slope(values):
    wide = values.astype(F32)
    return 1.0 - wide * wide


TILE = 512
CHUNK = 256


def trunk_back_kernel(
    factor,
    core_ref,
    kept_ref,
    theirs_ref,
    coeffs_ref,
    basis_ref,
    low_ref,
    high_ref,
    lead_ref,
    out_ref,
    mid_ref,
    other_ref,
    mine_ref,
    sum_mid,
    sum_out,
    sum_lead,
    sum_one,
    sum_two,
    delta_2,
    delta_1,
    delta_0,
):
    step = pl.program_id(0)
    width, tile = low_ref.shape
    basis = basis_ref.shape[0]
    scans = kept_ref.shape[0]

    @pl.when(step == 0)
    def _():
        for total in (sum_mid, sum_out, sum_lead, sum_one, sum_two):
            total[...] = jnp.zeros_like(total)

    def lanes(values):
        return functools.reduce(
            jnp.add, [values[:, at : at + 128] for at in range(0, tile, 128)]
        )

    plain, across = ((1,), (0,)), ((1,), (1,))
    for at in range(0, basis, CHUNK):
        rows = slice(at, at + CHUNK)
        pulled = dot(coeffs_ref[rows, :scans], kept_ref[...], plain)
        pulled += dot(coeffs_ref[rows, scans:], theirs_ref[...], plain)
        delta = factor * pulled * slope(basis_ref[rows, :])
        sum_two[rows, :] += lanes(delta)
        delta_2[rows, :] = delta.astype(BF)
    for at in range(0, width, CHUNK):
        rows = slice(at, at + CHUNK)
        delta = dot(out_ref[rows, :], delta_2[...], plain) * slope(high_ref[rows, :])
        sum_one[rows, :] += lanes(delta)
        delta_1[rows, :] = delta.astype(BF)
    for at in range(0, width, CHUNK):
        rows = slice(at, at + CHUNK)
        delta = dot(mid_ref[rows, :], delta_1[...], plain) * slope(low_ref[rows, :])
        delta_0[rows, :] = delta.astype(BF)
    for at in range(0, width, CHUNK):
        rows = slice(at, at + CHUNK)
        sum_out[rows, :] += dot(high_ref[rows, :], delta_2[...], across)
        sum_mid[rows, :] += dot(low_ref[rows, :], delta_1[...], across)
        sum_lead[rows, :] += dot(delta_0[rows, :], lead_ref[...], across)

    @pl.when(step == pl.num_programs(0) - 1)
    def _():
        lane = lax.broadcasted_iota(jnp.int32, (width, 128), 1)
        one = jnp.sum(sum_one[...], axis=1, keepdims=True)
        sum_lead[...] = jnp.where(lane == 5, one, sum_lead[...])
        two = jnp.sum(sum_two[...], axis=1, keepdims=True)
        sum_lead[:basis, :] = jnp.where(lane[:basis] == 6, two, sum_lead[:basis, :])
        core = core_ref[0]
        half = width // 2
        for target, start in ((other_ref, (1 - core) * half), (mine_ref, core * half)):
            rows = pl.ds(pl.multiple_of(start, half), half)
            at = 0
            for total in (sum_mid, sum_out, sum_lead):
                target[:, at : at + total.shape[1]] = total[rows, :].astype(target.dtype)
                at += total.shape[1]


def trunk_back(core, cotangent, theirs, coeffs, basis_vals, low, high, lead, out, mid, factor):
    width, half = low.shape
    basis = basis_vals.shape[0]
    scans = cotangent.shape[0]
    steps = half // TILE
    columns = width + basis + 128

    def whole(values):
        return pl.BlockSpec(values.shape, lambda i, c: (0, 0))

    def part(rows):
        return pl.BlockSpec((rows, TILE), lambda i, c: (0, i))

    product = 2 * half * (2 * scans * basis + 2 * width * basis + 2 * width * width + width * 128)
    return pl.pallas_call(
        functools.partial(trunk_back_kernel, factor),
        grid_spec=pltpu.PrefetchScalarGridSpec(
            num_scalar_prefetch=1,
            grid=(steps,),
            in_specs=[
                pl.BlockSpec((scans, TILE), lambda i, c: (0, c[0] * steps + i)),
                part(scans),
                whole(coeffs),
                part(basis),
                part(width),
                part(width),
                part(128),
                whole(out),
                whole(mid),
            ],
            out_specs=[pl.BlockSpec((width // 2, columns), lambda i, c: (0, 0))] * 2,
            scratch_shapes=[
                pltpu.VMEM((width, width), F32),
                pltpu.VMEM((width, basis), F32),
                pltpu.VMEM((width, 128), F32),
                pltpu.VMEM((width, 128), F32),
                pltpu.VMEM((basis, 128), F32),
                pltpu.VMEM((basis, TILE), BF),
                pltpu.VMEM((width, TILE), BF),
                pltpu.VMEM((width, TILE), BF),
            ],
        ),
        out_shape=[
            jax.ShapeDtypeStruct((width // 2, columns), BF),
            jax.ShapeDtypeStruct((width // 2, columns), F32),
        ],
        compiler_params=pltpu.CompilerParams(
            dimension_semantics=("arbitrary",), vmem_limit_bytes=48 * 1024 * 1024
        ),
        cost_estimate=pl.CostEstimate(
            flops=product, bytes_accessed=24 * 1024 * 1024, transcendentals=0
        ),
        name="trunk_back",
    )(core.reshape(1), cotangent, theirs, coeffs, basis_vals, low, high, lead, out, mid)


def on_device(
    cotangent,
    scan_paths,
    query_points,
    branch_in,
    branch_in_bias,
    branch_out,
    branch_out_bias,
    trunk_in,
    trunk_in_bias,
    trunk_mid,
    trunk_mid_bias,
    trunk_out,
    trunk_out_bias,
):
    core = lax.axis_index("core")
    scan_rows, point_cols = cotangent.shape
    half = point_cols // 2
    chips = lax.axis_size(CHIPS)
    pts = lax.axis_size(PTS)
    factor = 1.0 / math.sqrt(scan_rows * 4 * point_cols * pts)
    width = trunk_in.shape[1]
    basis = trunk_out.shape[1]

    zl = lax.axis_index("zl")
    sent = lax.dynamic_slice_in_dim(cotangent, (1 - core) * half, half, 1)
    pair_got = swap(jnp.concatenate([sent, scan_paths], axis=1), "core")
    points = lax.dynamic_slice_in_dim(query_points, core * half, half, 1)

    trunk_0 = dot(trunk_in, points, ((0,), (0,))) + trunk_in_bias[:, None]
    trunk_0 = jnp.tanh(trunk_0).astype(BF)
    trunk_1 = dot(trunk_mid[0], trunk_0, ((0,), (0,))) + trunk_mid_bias[0][:, None]
    trunk_1 = jnp.tanh(trunk_1).astype(BF)
    basis_vals = dot(trunk_out, trunk_1, ((0,), (0,))) + trunk_out_bias[:, None]
    basis_vals = jnp.tanh(basis_vals).astype(BF)

    local_paths = jnp.concatenate([scan_paths, pair_got[:, half:]], axis=0)
    side_paths = swap(local_paths, "zl")

    coef_theirs = dot(pair_got[:, :half], basis_vals, ((1,), (1,))).astype(BF)
    coef_swapped = swap(coef_theirs, "core")
    kept = lax.dynamic_slice_in_dim(cotangent, core * half, half, 1)
    coef_mine = dot(kept, basis_vals, ((1,), (1,)))

    hidden_local = tanh_layer(local_paths, branch_in, branch_in_bias)
    coeffs = dot(branch_out, hidden_local, ((0,), (1,))) + branch_out_bias[:, None]
    coeffs = coeffs.astype(BF)

    coef_part = (coef_mine + coef_swapped.astype(F32)).astype(BF)
    coef_part, coeffs, side_paths = lax.optimization_barrier((coef_part, coeffs, side_paths))
    coef_parts = exchange(coef_part.reshape(pts, scan_rows // pts, basis), PTS)

    lead = jnp.concatenate([points, jnp.ones((1, half), BF), jnp.zeros((123, half), BF)], axis=0)
    other, mine = trunk_back(
        core,
        cotangent,
        pair_got,
        coeffs,
        basis_vals,
        trunk_0,
        trunk_1,
        lead,
        trunk_out,
        trunk_mid[0],
        factor,
    )
    coef_parts, other = lax.optimization_barrier((coef_parts, other))
    coef_low = (factor * sum_parts(coef_parts)).astype(BF)

    pair = (mine + swap(other, "core").astype(F32)).astype(BF)
    columns = pair.shape[1]
    rows = width // 2 // chips
    coef_flat = jnp.concatenate([coef_low[:rows], coef_low[rows:]], axis=1)
    load = jnp.concatenate(
        [
            pair.reshape(chips, rows, columns),
            jnp.broadcast_to(coef_flat[None], (chips,) + coef_flat.shape),
        ],
        axis=2,
    )
    got = exchange(load, CHIPS)
    local = local_paths.reshape(2, scan_rows, -1)
    side = side_paths.reshape(2, scan_rows, -1)
    paths = jnp.where(
        zl == 0, jnp.stack([local, side], axis=1), jnp.stack([side, local], axis=1)
    ).reshape(4 * scan_rows, -1)
    hidden = tanh_layer(paths, branch_in, branch_in_bias)
    got, hidden = lax.optimization_barrier((got, hidden))
    total = sum_parts(got[:, :, :columns]).astype(BF)
    wide = jnp.broadcast_to(total[None], (chips, rows, columns))
    wide, got = lax.optimization_barrier((wide, got))
    spread = exchange(wide, CHIPS)

    coef_own = jnp.stack([got[:, :, columns : columns + basis], got[:, :, columns + basis :]], 1)
    coef_own = coef_own.reshape(2, scan_rows, basis)
    coef_other = swap(coef_own, "core")
    coef_all = jnp.stack([coef_own, coef_other]).reshape(4 * scan_rows, basis)
    grad_branch_out = rows_rows(hidden, coef_all)
    grad_branch_out_bias = jnp.sum(coef_all.astype(F32), axis=0)
    branch_delta = (dot(coef_all, branch_out, ((1,), (1,))) * slope(hidden)).astype(BF)
    grad_branch_in = rows_rows(paths, branch_delta)
    grad_branch_in_bias = jnp.sum(branch_delta.astype(F32), axis=0)

    spread, grad_branch_out, grad_branch_in = lax.optimization_barrier(
        (spread, grad_branch_out, grad_branch_in)
    )
    spread = spread.reshape(width // 2, columns)
    spread_theirs = swap(spread, "core")

    full = jnp.where(
        core == 0,
        jnp.concatenate([spread, spread_theirs], axis=0),
        jnp.concatenate([spread_theirs, spread], axis=0),
    ).astype(F32)
    tail = full[:, width + basis :]
    return (
        grad_branch_in,
        grad_branch_in_bias,
        grad_branch_out,
        grad_branch_out_bias,
        tail[:, :4].T,
        tail[:, 4],
        full[:, :width][None],
        tail[:, 5][None],
        full[:, width : width + basis],
        tail[:basis, 6],
    )


def solution(mesh):
    fine = Mesh(mesh.devices.reshape(2, 2, 4, 4, 2), ALL)
    scan, pts = ("zl", "core"), PTS
    placed = (P(scan, pts), P(scan, None), P(None, pts)) + (P(),) * 10
    return jax.shard_map(
        on_device, mesh=fine, in_specs=placed, out_specs=(P(),) * 10, check_vma=False
    )
```

```python
import functools
import math

import jax
import jax.numpy as jnp
from jax import lax
from jax.experimental import pallas as pl
from jax.experimental.pallas import tpu as pltpu
from jax.sharding import Mesh, PartitionSpec as P

ALL = ("zl", "core", "y", "x", "zh")
CHIPS = ("zl", "y", "x", "zh")
PTS = ("y", "x", "zh")
BF = jnp.bfloat16
F32 = jnp.float32


def dot(left, right, dims):
    return lax.dot_general(left, right, (dims, ((), ())), preferred_element_type=F32)


def rows_rows(left, right):
    return dot(left, right, ((0,), (0,)))


def swap(values, axis):
    return lax.ppermute(values, axis, [(0, 1), (1, 0)])


def exchange(values, axes):
    return lax.all_to_all(values, axes, split_axis=0, concat_axis=0, tiled=True)


def tanh_layer(inputs, weights, offsets):
    return jnp.tanh(dot(inputs, weights, ((1,), (0,))) + offsets).astype(BF)


def slope(values):
    wide = values.astype(F32)
    return 1.0 - wide * wide


TILE = 512
CHUNK = 256


def trunk_back_kernel(
    factor,
    core_ref,
    kept_ref,
    theirs_ref,
    coeffs_ref,
    basis_ref,
    low_ref,
    high_ref,
    lead_ref,
    out_ref,
    mid_ref,
    other_ref,
    mine_ref,
    sum_mid,
    sum_out,
    sum_lead,
    sum_one,
    sum_two,
    delta_2,
    delta_1,
    delta_0,
):
    step = pl.program_id(0)
    width, tile = low_ref.shape
    basis = basis_ref.shape[0]
    scans = kept_ref.shape[0]

    @pl.when(step == 0)
    def _():
        for total in (sum_mid, sum_out, sum_lead, sum_one, sum_two):
            total[...] = jnp.zeros_like(total)

    def lanes(values):
        return functools.reduce(
            jnp.add, [values[:, at : at + 128] for at in range(0, tile, 128)]
        )

    plain, across = ((1,), (0,)), ((1,), (1,))
    for at in range(0, basis, CHUNK):
        rows = slice(at, at + CHUNK)
        pulled = dot(coeffs_ref[rows, :scans], kept_ref[...], plain)
        pulled += dot(coeffs_ref[rows, scans:], theirs_ref[...], plain)
        delta = factor * pulled * slope(basis_ref[rows, :])
        sum_two[rows, :] += lanes(delta)
        delta_2[rows, :] = delta.astype(BF)
    for at in range(0, width, CHUNK):
        rows = slice(at, at + CHUNK)
        delta = dot(out_ref[rows, :], delta_2[...], plain) * slope(high_ref[rows, :])
        sum_one[rows, :] += lanes(delta)
        delta_1[rows, :] = delta.astype(BF)
    for at in range(0, width, CHUNK):
        rows = slice(at, at + CHUNK)
        delta = dot(mid_ref[rows, :], delta_1[...], plain) * slope(low_ref[rows, :])
        delta_0[rows, :] = delta.astype(BF)
    for at in range(0, width, CHUNK):
        rows = slice(at, at + CHUNK)
        sum_out[rows, :] += dot(high_ref[rows, :], delta_2[...], across)
        sum_mid[rows, :] += dot(low_ref[rows, :], delta_1[...], across)
        sum_lead[rows, :] += dot(delta_0[rows, :], lead_ref[...], across)

    @pl.when(step == pl.num_programs(0) - 1)
    def _():
        lane = lax.broadcasted_iota(jnp.int32, (width, 128), 1)
        one = jnp.sum(sum_one[...], axis=1, keepdims=True)
        sum_lead[...] = jnp.where(lane == 5, one, sum_lead[...])
        two = jnp.sum(sum_two[...], axis=1, keepdims=True)
        sum_lead[:basis, :] = jnp.where(lane[:basis] == 6, two, sum_lead[:basis, :])
        core = core_ref[0]
        half = width // 2
        for target, start in ((other_ref, (1 - core) * half), (mine_ref, core * half)):
            rows = pl.ds(pl.multiple_of(start, half), half)
            at = 0
            for total in (sum_mid, sum_out, sum_lead):
                target[:, at : at + total.shape[1]] = total[rows, :].astype(target.dtype)
                at += total.shape[1]


def trunk_back(core, cotangent, theirs, coeffs, basis_vals, low, high, lead, out, mid, factor):
    width, half = low.shape
    basis = basis_vals.shape[0]
    scans = cotangent.shape[0]
    steps = half // TILE
    columns = width + basis + 128

    def whole(values):
        return pl.BlockSpec(values.shape, lambda i, c: (0, 0))

    def part(rows):
        return pl.BlockSpec((rows, TILE), lambda i, c: (0, i))

    product = 2 * half * (2 * scans * basis + 2 * width * basis + 2 * width * width + width * 128)
    return pl.pallas_call(
        functools.partial(trunk_back_kernel, factor),
        grid_spec=pltpu.PrefetchScalarGridSpec(
            num_scalar_prefetch=1,
            grid=(steps,),
            in_specs=[
                pl.BlockSpec((scans, TILE), lambda i, c: (0, c[0] * steps + i)),
                part(scans),
                whole(coeffs),
                part(basis),
                part(width),
                part(width),
                part(128),
                whole(out),
                whole(mid),
            ],
            out_specs=[pl.BlockSpec((width // 2, columns), lambda i, c: (0, 0))] * 2,
            scratch_shapes=[
                pltpu.VMEM((width, width), F32),
                pltpu.VMEM((width, basis), F32),
                pltpu.VMEM((width, 128), F32),
                pltpu.VMEM((width, 128), F32),
                pltpu.VMEM((basis, 128), F32),
                pltpu.VMEM((basis, TILE), BF),
                pltpu.VMEM((width, TILE), BF),
                pltpu.VMEM((width, TILE), BF),
            ],
        ),
        out_shape=[
            jax.ShapeDtypeStruct((width // 2, columns), BF),
            jax.ShapeDtypeStruct((width // 2, columns), F32),
        ],
        compiler_params=pltpu.CompilerParams(
            dimension_semantics=("arbitrary",), vmem_limit_bytes=60 * 1024 * 1024
        ),
        cost_estimate=pl.CostEstimate(
            flops=product, bytes_accessed=24 * 1024 * 1024, transcendentals=0
        ),
        name="trunk_back",
    )(core.reshape(1), cotangent, theirs, coeffs, basis_vals, low, high, lead, out, mid)


def call(kernel, grid, ins, outs, shapes, scratch, flops, moved, limit=60):
    return pl.pallas_call(
        kernel,
        grid_spec=pltpu.PrefetchScalarGridSpec(
            num_scalar_prefetch=1, grid=(grid,), in_specs=ins, out_specs=outs, scratch_shapes=scratch
        ),
        out_shape=shapes,
        compiler_params=pltpu.CompilerParams(
            dimension_semantics=("arbitrary",), vmem_limit_bytes=limit * 1024 * 1024
        ),
        cost_estimate=pl.CostEstimate(flops=flops, bytes_accessed=moved, transcendentals=0),
    )


def head_kernel(
    core_ref,
    kept_ref,
    theirs_ref,
    high_ref,
    out_ref,
    bias_ref,
    basis_ref,
    coef_ref,
    flipped,
    column,
    mine,
    other,
):
    step = pl.program_id(0)
    scans = kept_ref.shape[0]
    basis = basis_ref.shape[0]

    @pl.when(step == 0)
    def _():
        flipped[...] = out_ref[...].T
        column[...] = jnp.broadcast_to(bias_ref[...], (128, basis)).T
        mine[...] = jnp.zeros_like(mine)
        other[...] = jnp.zeros_like(other)

    for at in range(0, basis, CHUNK):
        rows = slice(at, at + CHUNK)
        summed = dot(flipped[rows, :], high_ref[...], ((1,), (0,))) + column[rows, :1]
        basis_ref[rows, :] = jnp.tanh(summed).astype(BF)
    for at in range(0, basis, CHUNK):
        rows = slice(at, at + CHUNK)
        mine[:, rows] += dot(kept_ref[...], basis_ref[rows, :], ((1,), (1,)))
        other[:, rows] += dot(theirs_ref[...], basis_ref[rows, :], ((1,), (1,)))

    @pl.when(step == pl.num_programs(0) - 1)
    def _():
        core = core_ref[0]
        coef_ref[pl.ds(pl.multiple_of(core * scans, scans), scans), :] = mine[...].astype(BF)
        coef_ref[pl.ds(pl.multiple_of((1 - core) * scans, scans), scans), :] = other[...].astype(BF)


def trunk_head(core, cotangent, theirs, high, out, bias):
    width, half = high.shape
    basis = out.shape[1]
    scans = cotangent.shape[0]
    steps = half // TILE
    return call(
        head_kernel,
        steps,
        [
            pl.BlockSpec((scans, TILE), lambda i, c: (0, c[0] * steps + i)),
            pl.BlockSpec((scans, TILE), lambda i, c: (0, i)),
            pl.BlockSpec((width, TILE), lambda i, c: (0, i)),
            pl.BlockSpec((width, basis), lambda i, c: (0, 0)),
            pl.BlockSpec((1, basis), lambda i, c: (0, 0)),
        ],
        [
            pl.BlockSpec((basis, TILE), lambda i, c: (0, i)),
            pl.BlockSpec((2 * scans, basis), lambda i, c: (0, 0)),
        ],
        [
            jax.ShapeDtypeStruct((basis, half), BF),
            jax.ShapeDtypeStruct((2 * scans, basis), BF),
        ],
        [
            pltpu.VMEM((basis, width), BF),
            pltpu.VMEM((basis, 128), F32),
            pltpu.VMEM((scans, basis), F32),
            pltpu.VMEM((scans, basis), F32),
        ],
        2 * half * basis * (width + 2 * scans),
        14 * 1024 * 1024,
    )(core.reshape(1), cotangent, theirs, high, out, bias.reshape(1, basis))


def load_kernel(factor, core_ref, parts_ref, mine_ref, swapped_ref, load_ref, coef):
    columns = mine_ref.shape[1]
    basis = parts_ref.shape[1]

    @pl.when(pl.program_id(0) == 0)
    def _():
        total = jnp.zeros((16, basis), F32)
        for at in range(0, parts_ref.shape[0], 16):
            total += parts_ref[at : at + 16, :].astype(F32)
        total = total * factor
        flat = jnp.concatenate([total[:8], total[8:]], axis=1)
        coef[...] = jnp.concatenate([flat, flat], axis=0).astype(BF)

    load_ref[:, :columns] = (mine_ref[...] + swapped_ref[...].astype(F32)).astype(BF)
    for at in range(0, load_ref.shape[0], 16):
        load_ref[at : at + 16, columns:] = coef[...]


def pack_load(core, parts, mine, swapped, factor):
    rows, columns = mine.shape
    basis = parts.shape[1]
    tile = 128
    return call(
        functools.partial(load_kernel, factor),
        rows // tile,
        [
            pl.BlockSpec(parts.shape, lambda i, c: (0, 0)),
            pl.BlockSpec((tile, columns), lambda i, c: (i, 0)),
            pl.BlockSpec((tile, columns), lambda i, c: (i, 0)),
        ],
        pl.BlockSpec((tile, columns + 2 * basis), lambda i, c: (i, 0)),
        jax.ShapeDtypeStruct((rows, columns + 2 * basis), BF),
        [pltpu.VMEM((16, 2 * basis), BF)],
        0,
        9 * 1024 * 1024,
    )(core.reshape(1), parts, mine, swapped)


def total_kernel(core_ref, got_ref, wide_ref, coef_ref):
    rows, columns = wide_ref.shape
    total = jnp.zeros((16, columns), F32)
    for at in range(0, rows, 16):
        total += got_ref[at : at + 16, :columns].astype(F32)
        coef_ref[at : at + 16, :] = got_ref[at : at + 16, columns:]
    total = total[:8] + total[8:]
    both = jnp.concatenate([total, total], axis=0).astype(BF)
    for at in range(0, rows, 16):
        wide_ref[at : at + 16, :] = both


def sum_spread(core, got, columns):
    rows, wide = got.shape
    return call(
        total_kernel,
        1,
        [pl.BlockSpec((rows, wide), lambda i, c: (0, 0))],
        [
            pl.BlockSpec((rows, columns), lambda i, c: (0, 0)),
            pl.BlockSpec((rows, wide - columns), lambda i, c: (0, 0)),
        ],
        [
            jax.ShapeDtypeStruct((rows, columns), BF),
            jax.ShapeDtypeStruct((rows, wide - columns), BF),
        ],
        [],
        0,
        2 * rows * wide * 2,
    )(core.reshape(1), got)


def unpack_kernel(core_ref, own_ref, *refs):
    mid_ref, out_ref, in_ref, zero_ref, one_ref, two_ref = refs[-6:]
    width, basis = mid_ref.shape[1], out_ref.shape[1]
    mid_ref[...] = own_ref[:, :width].astype(F32)
    out_ref[...] = own_ref[:, width : width + basis].astype(F32)
    small = own_ref[:, width + basis :].astype(F32).T
    in_ref[...] = small[:4]
    zero_ref[...] = small[4:5]
    one_ref[...] = small[5:6]
    two_ref[...] = small[6:7]


def unpack(side, own, width, basis, earlier=()):
    rows, columns = own.shape
    tile = 256
    steps = rows // tile

    def row(i, c):
        return (c[0] * steps + i, 0)

    def lane(i, c):
        return (0, c[0] * steps + i)

    return pl.pallas_call(
        unpack_kernel,
        grid_spec=pltpu.PrefetchScalarGridSpec(
            num_scalar_prefetch=1,
            grid=(steps,),
            in_specs=[pl.BlockSpec((tile, columns), lambda i, c: (i, 0))]
            + [pl.BlockSpec(memory_space=pl.ANY)] * len(earlier),
            out_specs=[
                pl.BlockSpec((tile, width), row),
                pl.BlockSpec((tile, basis), row),
                pl.BlockSpec((4, tile), lane),
                pl.BlockSpec((1, tile), lane),
                pl.BlockSpec((1, tile), lane),
                pl.BlockSpec((1, tile), lane),
            ],
        ),
        out_shape=[
            jax.ShapeDtypeStruct((width, width), F32),
            jax.ShapeDtypeStruct((width, basis), F32),
            jax.ShapeDtypeStruct((4, width), F32),
            jax.ShapeDtypeStruct((1, width), F32),
            jax.ShapeDtypeStruct((1, width), F32),
            jax.ShapeDtypeStruct((1, width), F32),
        ],
        input_output_aliases={2 + at: at for at in range(len(earlier))},
        compiler_params=pltpu.CompilerParams(
            dimension_semantics=("arbitrary",), vmem_limit_bytes=60 * 1024 * 1024
        ),
        cost_estimate=pl.CostEstimate(
            flops=0, bytes_accessed=5 * 1024 * 1024, transcendentals=0
        ),
    )(side.reshape(1), own, *earlier)


def on_device(
    cotangent,
    scan_paths,
    query_points,
    branch_in,
    branch_in_bias,
    branch_out,
    branch_out_bias,
    trunk_in,
    trunk_in_bias,
    trunk_mid,
    trunk_mid_bias,
    trunk_out,
    trunk_out_bias,
):
    core = lax.axis_index("core")
    scan_rows, point_cols = cotangent.shape
    half = point_cols // 2
    chips = lax.axis_size(CHIPS)
    pts = lax.axis_size(PTS)
    factor = 1.0 / math.sqrt(scan_rows * 4 * point_cols * pts)
    width = trunk_in.shape[1]
    basis = trunk_out.shape[1]

    zl = lax.axis_index("zl")
    theirs = swap(lax.dynamic_slice_in_dim(cotangent, (1 - core) * half, half, 1), "core")
    pair_paths = swap(scan_paths, "core")
    points = lax.dynamic_slice_in_dim(query_points, core * half, half, 1)

    trunk_0 = dot(trunk_in, points, ((0,), (0,))) + trunk_in_bias[:, None]
    trunk_0 = jnp.tanh(trunk_0).astype(BF)
    trunk_1 = dot(trunk_mid[0], trunk_0, ((0,), (0,))) + trunk_mid_bias[0][:, None]
    trunk_1 = jnp.tanh(trunk_1).astype(BF)
    basis_vals, coef_part = trunk_head(
        core, cotangent, theirs, trunk_1, trunk_out, trunk_out_bias
    )

    local_paths = jnp.concatenate([scan_paths, pair_paths], axis=0)
    side_paths = swap(local_paths, "zl")

    hidden_local = tanh_layer(local_paths, branch_in, branch_in_bias)
    coeffs = dot(branch_out, hidden_local, ((0,), (1,))) + branch_out_bias[:, None]
    coeffs = coeffs.astype(BF)

    coef_part, coeffs = lax.optimization_barrier((coef_part, coeffs))
    coef_parts = exchange(coef_part, ("core",) + PTS)

    lead = jnp.concatenate([points, jnp.ones((1, half), BF), jnp.zeros((123, half), BF)], axis=0)
    other, mine = trunk_back(
        core,
        cotangent,
        theirs,
        coeffs,
        basis_vals,
        trunk_0,
        trunk_1,
        lead,
        trunk_out,
        trunk_mid[0],
        factor,
    )
    coef_parts, side_paths, other = lax.optimization_barrier((coef_parts, side_paths, other))

    columns = mine.shape[1]
    load = pack_load(core, coef_parts, mine, swap(other, "core"), factor)
    got = exchange(load, CHIPS)
    local = local_paths.reshape(2, scan_rows, -1)
    side = side_paths.reshape(2, scan_rows, -1)
    paths = jnp.where(
        zl == 0, jnp.stack([local, side], axis=1), jnp.stack([side, local], axis=1)
    ).reshape(4 * scan_rows, -1)
    hidden = tanh_layer(paths, branch_in, branch_in_bias)
    got, hidden = lax.optimization_barrier((got, hidden))
    wide, coef_own = sum_spread(core, got, columns)
    spread = exchange(wide, CHIPS)

    coef_all = jnp.stack([coef_own, swap(coef_own, "core")])
    rows = coef_own.shape[0] // chips
    coef_all = coef_all.reshape(2, chips, rows, 2, basis).transpose(0, 1, 3, 2, 4)
    coef_all = coef_all.reshape(4 * scan_rows, basis)
    grad_branch_out = rows_rows(hidden, coef_all)
    grad_branch_out_bias = jnp.sum(coef_all.astype(F32), axis=0)
    branch_delta = (dot(coef_all, branch_out, ((1,), (1,))) * slope(hidden)).astype(BF)
    grad_branch_in = rows_rows(paths, branch_delta)
    grad_branch_in_bias = jnp.sum(branch_delta.astype(F32), axis=0)

    spread, grad_branch_out, grad_branch_in, grad_branch_out_bias = lax.optimization_barrier(
        (spread, grad_branch_out, grad_branch_in, grad_branch_out_bias)
    )
    spread_theirs = swap(spread, "core")
    first = unpack(core, spread, width, basis)
    grad_mid, grad_out, grad_in, bias_0, bias_1, bias_2 = unpack(
        1 - core, spread_theirs, width, basis, first
    )
    return (
        grad_branch_in,
        grad_branch_in_bias,
        grad_branch_out,
        grad_branch_out_bias,
        grad_in,
        bias_0[0],
        grad_mid[None],
        bias_1,
        grad_out,
        bias_2[0, :basis],
    )


def solution(mesh):
    fine = Mesh(mesh.devices.reshape(2, 2, 4, 4, 2), ALL)
    scan, pts = ("zl", "core"), PTS
    placed = (P(scan, pts), P(scan, None), P(None, pts)) + (P(),) * 10
    return jax.shard_map(
        on_device, mesh=fine, in_specs=placed, out_specs=(P(),) * 10, check_vma=False
    )
```

```python
import functools
import math

import jax
import jax.numpy as jnp
from jax import lax
from jax.experimental import pallas as pl
from jax.experimental.pallas import tpu as pltpu
from jax.sharding import Mesh, PartitionSpec as P

ALL = ("zl", "core", "y", "x", "zh")
CHIPS = ("zl", "y", "x", "zh")
PTS = ("y", "x", "zh")
BF = jnp.bfloat16
F32 = jnp.float32


def dot(left, right, dims):
    return lax.dot_general(left, right, (dims, ((), ())), preferred_element_type=F32)


def rows_rows(left, right):
    return dot(left, right, ((0,), (0,)))


def swap(values, axis):
    return lax.ppermute(values, axis, [(0, 1), (1, 0)])


def exchange(values, axes):
    return lax.all_to_all(values, axes, split_axis=0, concat_axis=0, tiled=True)


def tanh_layer(inputs, weights, offsets):
    return jnp.tanh(dot(inputs, weights, ((1,), (0,))) + offsets).astype(BF)


def slope(values):
    wide = values.astype(F32)
    return 1.0 - wide * wide


TILE = 512
ROOM = 60
CHUNK = 256


def trunk_back_kernel(
    factor,
    core_ref,
    kept_ref,
    theirs_ref,
    coeffs_ref,
    basis_ref,
    low_ref,
    high_ref,
    points_ref,
    out_ref,
    mid_ref,
    other_ref,
    mine_ref,
    sum_mid,
    sum_out,
    sum_lead,
    sum_one,
    sum_two,
    delta_2,
    delta_1,
    delta_0,
    lead,
):
    step = pl.program_id(0)
    width, tile = low_ref.shape
    basis = basis_ref.shape[0]
    scans = kept_ref.shape[0]

    @pl.when(step == 0)
    def _():
        for total in (sum_mid, sum_out, sum_lead, sum_one, sum_two):
            total[...] = jnp.zeros_like(total)
        lead[...] = jnp.zeros_like(lead)

    ones, blank = jnp.ones((1, tile), F32), jnp.zeros((11, tile), F32)
    lead[:16, :] = jnp.concatenate([points_ref[...].astype(F32), ones, blank], axis=0).astype(BF)

    def lanes(values):
        return functools.reduce(
            jnp.add, [values[:, at : at + 128] for at in range(0, tile, 128)]
        )

    plain, across = ((1,), (0,)), ((1,), (1,))
    for at in range(0, basis, CHUNK):
        rows = slice(at, at + CHUNK)
        pulled = dot(coeffs_ref[rows, :scans], kept_ref[...], plain)
        pulled += dot(coeffs_ref[rows, scans:], theirs_ref[...], plain)
        delta = factor * pulled * slope(basis_ref[rows, :])
        sum_two[rows, :] += lanes(delta)
        delta_2[rows, :] = delta.astype(BF)
    for at in range(0, width, CHUNK):
        rows = slice(at, at + CHUNK)
        delta = dot(out_ref[rows, :], delta_2[...], plain) * slope(high_ref[rows, :])
        sum_one[rows, :] += lanes(delta)
        delta_1[rows, :] = delta.astype(BF)
    for at in range(0, width, CHUNK):
        rows = slice(at, at + CHUNK)
        delta = dot(mid_ref[rows, :], delta_1[...], plain) * slope(low_ref[rows, :])
        delta_0[rows, :] = delta.astype(BF)
    for at in range(0, width, CHUNK):
        rows = slice(at, at + CHUNK)
        sum_out[rows, :] += dot(high_ref[rows, :], delta_2[...], across)
        sum_mid[rows, :] += dot(low_ref[rows, :], delta_1[...], across)
        sum_lead[rows, :] += dot(delta_0[rows, :], lead[...], across)

    @pl.when(step == pl.num_programs(0) - 1)
    def _():
        lane = lax.broadcasted_iota(jnp.int32, (width, 128), 1)
        one = jnp.sum(sum_one[...], axis=1, keepdims=True)
        sum_lead[...] = jnp.where(lane == 5, one, sum_lead[...])
        two = jnp.sum(sum_two[...], axis=1, keepdims=True)
        sum_lead[:basis, :] = jnp.where(lane[:basis] == 6, two, sum_lead[:basis, :])
        core = core_ref[0]
        half = width // 2
        for target, start in ((other_ref, (1 - core) * half), (mine_ref, core * half)):
            rows = pl.ds(pl.multiple_of(start, half), half)
            at = 0
            for total in (sum_mid, sum_out, sum_lead):
                target[:, at : at + total.shape[1]] = total[rows, :].astype(target.dtype)
                at += total.shape[1]


def trunk_back(core, cotangent, theirs, coeffs, basis_vals, low, high, points, out, mid, factor):
    width, half = low.shape
    basis = basis_vals.shape[0]
    scans = cotangent.shape[0]
    steps = half // TILE
    columns = width + basis + 128

    def whole(values):
        return pl.BlockSpec(values.shape, lambda i, c: (0, 0), pipeline_mode=pl.Buffered(1))

    def part(rows):
        return pl.BlockSpec((rows, TILE), lambda i, c: (0, i))

    product = 2 * half * (2 * scans * basis + 2 * width * basis + 2 * width * width + width * 128)
    return pl.pallas_call(
        functools.partial(trunk_back_kernel, factor),
        grid_spec=pltpu.PrefetchScalarGridSpec(
            num_scalar_prefetch=1,
            grid=(steps,),
            in_specs=[
                pl.BlockSpec((scans, TILE), lambda i, c: (0, c[0] * steps + i)),
                part(scans),
                whole(coeffs),
                part(basis),
                part(width),
                part(width),
                pl.BlockSpec((points.shape[0], TILE), lambda i, c: (0, c[0] * steps + i)),
                whole(out),
                whole(mid),
            ],
            out_specs=[pl.BlockSpec((width // 2, columns), lambda i, c: (0, 0))] * 2,
            scratch_shapes=[
                pltpu.VMEM((width, width), F32),
                pltpu.VMEM((width, basis), F32),
                pltpu.VMEM((width, 128), F32),
                pltpu.VMEM((width, 128), F32),
                pltpu.VMEM((basis, 128), F32),
                pltpu.VMEM((basis, TILE), BF),
                pltpu.VMEM((width, TILE), BF),
                pltpu.VMEM((width, TILE), BF),
                pltpu.VMEM((128, TILE), BF),
            ],
        ),
        out_shape=[
            jax.ShapeDtypeStruct((width // 2, columns), BF),
            jax.ShapeDtypeStruct((width // 2, columns), BF),
        ],
        compiler_params=pltpu.CompilerParams(
            dimension_semantics=("arbitrary",), vmem_limit_bytes=ROOM * 1024 * 1024
        ),
        cost_estimate=pl.CostEstimate(
            flops=product, bytes_accessed=24 * 1024 * 1024, transcendentals=0
        ),
        name="trunk_back",
    )(core.reshape(1), cotangent, theirs, coeffs, basis_vals, low, high, points, out, mid)


def call(kernel, grid, ins, outs, shapes, scratch, flops, moved, limit=ROOM):
    return pl.pallas_call(
        kernel,
        grid_spec=pltpu.PrefetchScalarGridSpec(
            num_scalar_prefetch=1, grid=(grid,), in_specs=ins, out_specs=outs, scratch_shapes=scratch
        ),
        out_shape=shapes,
        compiler_params=pltpu.CompilerParams(
            dimension_semantics=("arbitrary",), vmem_limit_bytes=limit * 1024 * 1024
        ),
        cost_estimate=pl.CostEstimate(flops=flops, bytes_accessed=moved, transcendentals=0),
    )


def head_kernel(
    core_ref,
    kept_ref,
    theirs_ref,
    high_ref,
    out_ref,
    bias_ref,
    basis_ref,
    coef_ref,
    flipped,
    column,
    mine,
    other,
):
    step = pl.program_id(0)
    scans = kept_ref.shape[0]
    basis = basis_ref.shape[0]

    @pl.when(step == 0)
    def _():
        flipped[...] = out_ref[...].T
        column[...] = jnp.broadcast_to(bias_ref[...], (128, basis)).T
        mine[...] = jnp.zeros_like(mine)
        other[...] = jnp.zeros_like(other)

    for at in range(0, basis, CHUNK):
        rows = slice(at, at + CHUNK)
        summed = dot(flipped[rows, :], high_ref[...], ((1,), (0,))) + column[rows, :1]
        basis_ref[rows, :] = jnp.tanh(summed).astype(BF)
    for at in range(0, basis, CHUNK):
        rows = slice(at, at + CHUNK)
        mine[:, rows] += dot(kept_ref[...], basis_ref[rows, :], ((1,), (1,)))
        other[:, rows] += dot(theirs_ref[...], basis_ref[rows, :], ((1,), (1,)))

    @pl.when(step == pl.num_programs(0) - 1)
    def _():
        core = core_ref[0]
        coef_ref[pl.ds(pl.multiple_of(core * scans, scans), scans), :] = mine[...].astype(BF)
        coef_ref[pl.ds(pl.multiple_of((1 - core) * scans, scans), scans), :] = other[...].astype(BF)


def trunk_head(core, cotangent, theirs, high, out, bias):
    width, half = high.shape
    basis = out.shape[1]
    scans = cotangent.shape[0]
    steps = half // TILE
    return call(
        head_kernel,
        steps,
        [
            pl.BlockSpec((scans, TILE), lambda i, c: (0, c[0] * steps + i)),
            pl.BlockSpec((scans, TILE), lambda i, c: (0, i)),
            pl.BlockSpec((width, TILE), lambda i, c: (0, i)),
            pl.BlockSpec((width, basis), lambda i, c: (0, 0)),
            pl.BlockSpec((1, basis), lambda i, c: (0, 0)),
        ],
        [
            pl.BlockSpec((basis, TILE), lambda i, c: (0, i)),
            pl.BlockSpec((2 * scans, basis), lambda i, c: (0, 0)),
        ],
        [
            jax.ShapeDtypeStruct((basis, half), BF),
            jax.ShapeDtypeStruct((2 * scans, basis), BF),
        ],
        [
            pltpu.VMEM((basis, width), BF),
            pltpu.VMEM((basis, 128), F32),
            pltpu.VMEM((scans, basis), F32),
            pltpu.VMEM((scans, basis), F32),
        ],
        2 * half * basis * (width + 2 * scans),
        14 * 1024 * 1024,
    )(core.reshape(1), cotangent, theirs, high, out, bias.reshape(1, basis))


def load_kernel(factor, core_ref, parts_ref, mine_ref, swapped_ref, load_ref, coef):
    columns = mine_ref.shape[1]
    basis = parts_ref.shape[1]

    @pl.when(pl.program_id(0) == 0)
    def _():
        total = jnp.zeros((16, basis), F32)
        for at in range(0, parts_ref.shape[0], 16):
            total += parts_ref[at : at + 16, :].astype(F32)
        total = total * factor
        flat = jnp.concatenate([total[:8], total[8:]], axis=1)
        coef[...] = jnp.concatenate([flat, flat], axis=0).astype(BF)

    load_ref[:, :columns] = (mine_ref[...].astype(F32) + swapped_ref[...].astype(F32)).astype(BF)
    for at in range(0, load_ref.shape[0], 16):
        load_ref[at : at + 16, columns:] = coef[...]


def pack_load(core, parts, mine, swapped, factor):
    rows, columns = mine.shape
    basis = parts.shape[1]
    tile = 256
    return call(
        functools.partial(load_kernel, factor),
        rows // tile,
        [
            pl.BlockSpec(parts.shape, lambda i, c: (0, 0)),
            pl.BlockSpec((tile, columns), lambda i, c: (i, 0)),
            pl.BlockSpec((tile, columns), lambda i, c: (i, 0)),
        ],
        pl.BlockSpec((tile, columns + 2 * basis), lambda i, c: (i, 0)),
        jax.ShapeDtypeStruct((rows, columns + 2 * basis), BF),
        [pltpu.VMEM((16, 2 * basis), BF)],
        0,
        9 * 1024 * 1024,
    )(core.reshape(1), parts, mine, swapped)


def total_kernel(core_ref, got_ref, wide_ref, coef_ref):
    rows, columns = wide_ref.shape
    total = jnp.zeros((16, columns), F32)
    for at in range(0, rows, 16):
        total += got_ref[at : at + 16, :columns].astype(F32)
        coef_ref[at : at + 16, :] = got_ref[at : at + 16, columns:]
    total = total[:8] + total[8:]
    both = jnp.concatenate([total, total], axis=0).astype(BF)
    for at in range(0, rows, 16):
        wide_ref[at : at + 16, :] = both


def sum_spread(core, got, columns):
    rows, wide = got.shape
    return call(
        total_kernel,
        1,
        [pl.BlockSpec((rows, wide), lambda i, c: (0, 0))],
        [
            pl.BlockSpec((rows, columns), lambda i, c: (0, 0)),
            pl.BlockSpec((rows, wide - columns), lambda i, c: (0, 0)),
        ],
        [
            jax.ShapeDtypeStruct((rows, columns), BF),
            jax.ShapeDtypeStruct((rows, wide - columns), BF),
        ],
        [],
        0,
        2 * rows * wide * 2,
    )(core.reshape(1), got)


def unpack_kernel(core_ref, own_ref, *refs):
    mid_ref, out_ref, in_ref, zero_ref, one_ref, two_ref = refs[-6:]
    width, basis = mid_ref.shape[1], out_ref.shape[1]
    mid_ref[...] = own_ref[:, :width].astype(F32)
    out_ref[...] = own_ref[:, width : width + basis].astype(F32)
    small = own_ref[:, width + basis :].astype(F32).T
    in_ref[...] = small[:4]
    zero_ref[...] = small[4:5]
    one_ref[...] = small[5:6]
    kept = refs[5][...] if len(refs) > 6 else small[6:7]
    two_ref[...] = jnp.where(core_ref[0] == 0, small[6:7], kept)


def unpack(side, own, width, basis, earlier=()):
    rows, columns = own.shape
    tile = 256
    steps = rows // tile

    def row(i, c):
        return (c[0] * steps + i, 0)

    def lane(i, c):
        return (0, c[0] * steps + i)

    return pl.pallas_call(
        unpack_kernel,
        grid_spec=pltpu.PrefetchScalarGridSpec(
            num_scalar_prefetch=1,
            grid=(steps,),
            in_specs=[pl.BlockSpec((tile, columns), lambda i, c: (i, 0))]
            + [pl.BlockSpec(memory_space=pl.ANY)] * (len(earlier) - 1)
            + [pl.BlockSpec((1, tile), lambda i, c: (0, i))] * (len(earlier) > 0),
            out_specs=[
                pl.BlockSpec((tile, width), row),
                pl.BlockSpec((tile, basis), row),
                pl.BlockSpec((4, tile), lane),
                pl.BlockSpec((1, tile), lane),
                pl.BlockSpec((1, tile), lane),
                pl.BlockSpec((1, tile), lambda i, c: (0, i)),
            ],
        ),
        out_shape=[
            jax.ShapeDtypeStruct((width, width), F32),
            jax.ShapeDtypeStruct((width, basis), F32),
            jax.ShapeDtypeStruct((4, width), F32),
            jax.ShapeDtypeStruct((1, width), F32),
            jax.ShapeDtypeStruct((1, width), F32),
            jax.ShapeDtypeStruct((1, basis), F32),
        ],
        input_output_aliases={2 + at: at for at in range(len(earlier))},
        compiler_params=pltpu.CompilerParams(
            dimension_semantics=("arbitrary",), vmem_limit_bytes=16 * 1024 * 1024
        ),
        cost_estimate=pl.CostEstimate(
            flops=0, bytes_accessed=5 * 1024 * 1024, transcendentals=0
        ),
    )(side.reshape(1), own, *earlier)


def on_device(
    cotangent,
    scan_paths,
    query_points,
    branch_in,
    branch_in_bias,
    branch_out,
    branch_out_bias,
    trunk_in,
    trunk_in_bias,
    trunk_mid,
    trunk_mid_bias,
    trunk_out,
    trunk_out_bias,
):
    core = lax.axis_index("core")
    scan_rows, point_cols = cotangent.shape
    half = point_cols // 2
    chips = lax.axis_size(CHIPS)
    pts = lax.axis_size(PTS)
    factor = 1.0 / math.sqrt(scan_rows * 4 * point_cols * pts)
    width = trunk_in.shape[1]
    basis = trunk_out.shape[1]

    theirs = swap(lax.dynamic_slice_in_dim(cotangent, (1 - core) * half, half, 1), "core")
    pair_paths = swap(scan_paths, "core")
    zl = lax.axis_index("zl")
    points = lax.dynamic_slice_in_dim(query_points, core * half, half, 1)

    trunk_0 = dot(trunk_in, points, ((0,), (0,))) + trunk_in_bias[:, None]
    trunk_0 = jnp.tanh(trunk_0).astype(BF)
    trunk_1 = dot(trunk_mid[0], trunk_0, ((0,), (0,))) + trunk_mid_bias[0][:, None]
    trunk_1 = jnp.tanh(trunk_1).astype(BF)
    basis_vals, coef_part = trunk_head(
        core, cotangent, theirs, trunk_1, trunk_out, trunk_out_bias
    )

    local_paths = jnp.concatenate([scan_paths, pair_paths], axis=0)
    side_paths = swap(local_paths, "zl")

    hidden_local = tanh_layer(local_paths, branch_in, branch_in_bias)
    coeffs = dot(branch_out, hidden_local, ((0,), (1,))) + branch_out_bias[:, None]
    coeffs = coeffs.astype(BF)

    coef_part, coeffs = lax.optimization_barrier((coef_part, coeffs))
    coef_parts = exchange(coef_part, ("core",) + PTS)

    other, mine = trunk_back(
        core,
        cotangent,
        theirs,
        coeffs,
        basis_vals,
        trunk_0,
        trunk_1,
        query_points,
        trunk_out,
        trunk_mid[0],
        factor,
    )
    coef_parts, side_paths, other = lax.optimization_barrier((coef_parts, side_paths, other))

    columns = mine.shape[1]
    load = pack_load(core, coef_parts, mine, swap(other, "core"), factor)
    got = exchange(load, CHIPS)
    local = local_paths.reshape(2, scan_rows, -1)
    side = side_paths.reshape(2, scan_rows, -1)
    paths = jnp.where(
        zl == 0, jnp.stack([local, side], axis=1), jnp.stack([side, local], axis=1)
    ).reshape(4 * scan_rows, -1)
    hidden = tanh_layer(paths, branch_in, branch_in_bias)
    got, hidden = lax.optimization_barrier((got, hidden))
    wide, coef_own = sum_spread(core, got, columns)
    spread = exchange(wide, CHIPS)

    coef_all = jnp.stack([coef_own, swap(coef_own, "core")])
    rows = coef_own.shape[0] // chips
    coef_all = coef_all.reshape(2, chips, rows, 2, basis).transpose(0, 1, 3, 2, 4)
    coef_all = coef_all.reshape(4 * scan_rows, basis)
    grad_branch_out = rows_rows(hidden, coef_all)
    grad_branch_out_bias = jnp.sum(coef_all.astype(F32), axis=0)
    branch_delta = (dot(coef_all, branch_out, ((1,), (1,))) * slope(hidden)).astype(BF)
    grad_branch_in = rows_rows(paths, branch_delta)
    grad_branch_in_bias = jnp.sum(branch_delta.astype(F32), axis=0)

    spread, grad_branch_out, grad_branch_in, grad_branch_out_bias = lax.optimization_barrier(
        (spread, grad_branch_out, grad_branch_in, grad_branch_out_bias)
    )
    spread_theirs = swap(spread, "core")
    first = unpack(core, spread, width, basis)
    grad_mid, grad_out, grad_in, bias_0, bias_1, bias_2 = unpack(
        1 - core, spread_theirs, width, basis, first
    )
    return (
        grad_branch_in,
        grad_branch_in_bias,
        grad_branch_out,
        grad_branch_out_bias,
        grad_in,
        bias_0[0],
        grad_mid[None],
        bias_1,
        grad_out,
        bias_2[0],
    )


def solution(mesh):
    fine = Mesh(mesh.devices.reshape(2, 2, 4, 4, 2), ALL)
    scan, pts = ("zl", "core"), PTS
    placed = (P(scan, pts), P(scan, None), P(None, pts)) + (P(),) * 10
    return jax.shard_map(
        on_device, mesh=fine, in_specs=placed, out_specs=(P(),) * 10, check_vma=False
    )
```

```python
import functools
import math

import jax
import jax.numpy as jnp
from jax import lax
from jax.experimental import pallas as pl
from jax.experimental.pallas import tpu as pltpu
from jax.sharding import Mesh, PartitionSpec as P

ALL = ("zl", "core", "y", "x", "zh")
CHIPS = ("zl", "y", "x", "zh")
PTS = ("y", "x", "zh")
BF = jnp.bfloat16
F32 = jnp.float32


def dot(left, right, dims):
    return lax.dot_general(left, right, (dims, ((), ())), preferred_element_type=F32)


def rows_rows(left, right):
    return dot(left, right, ((0,), (0,)))


def swap(values, axis):
    return lax.ppermute(values, axis, [(0, 1), (1, 0)])


def exchange(values, axes):
    return lax.all_to_all(values, axes, split_axis=0, concat_axis=0, tiled=True)


def tanh_layer(inputs, weights, offsets):
    return jnp.tanh(dot(inputs, weights, ((1,), (0,))) + offsets).astype(BF)


def slope(values):
    wide = values.astype(F32)
    return 1.0 - wide * wide


TILE = 512
ROOM = 60
CHUNK = 256


def trunk_back_kernel(
    core_ref,
    delta_2,
    low_ref,
    high_ref,
    points_ref,
    out_ref,
    mid_ref,
    other_ref,
    mine_ref,
    sum_mid,
    sum_out,
    sum_lead,
    sum_one,
    sum_two,
    delta_1,
    delta_0,
    lead,
):
    step = pl.program_id(0)
    width, tile = low_ref.shape
    basis = delta_2.shape[0]

    @pl.when(step == 0)
    def _():
        for total in (sum_mid, sum_out, sum_lead, sum_one, sum_two):
            total[...] = jnp.zeros_like(total)
        lead[...] = jnp.zeros_like(lead)

    ones, blank = jnp.ones((1, tile), F32), jnp.zeros((11, tile), F32)
    lead[:16, :] = jnp.concatenate([points_ref[...].astype(F32), ones, blank], axis=0).astype(BF)

    def lanes(values):
        return functools.reduce(
            jnp.add, [values[:, at : at + 128] for at in range(0, tile, 128)]
        )

    plain, across = ((1,), (0,)), ((1,), (1,))
    sum_two[...] += lanes(delta_2[...].astype(F32))
    for at in range(0, width, CHUNK):
        rows = slice(at, at + CHUNK)
        delta = dot(out_ref[rows, :], delta_2[...], plain) * slope(high_ref[rows, :])
        sum_one[rows, :] += lanes(delta)
        delta_1[rows, :] = delta.astype(BF)
    for at in range(0, width, CHUNK):
        rows = slice(at, at + CHUNK)
        delta = dot(mid_ref[rows, :], delta_1[...], plain) * slope(low_ref[rows, :])
        delta_0[rows, :] = delta.astype(BF)
    for at in range(0, width, CHUNK):
        rows = slice(at, at + CHUNK)
        sum_out[rows, :] += dot(high_ref[rows, :], delta_2[...], across)
        sum_mid[rows, :] += dot(low_ref[rows, :], delta_1[...], across)
        sum_lead[rows, :] += dot(delta_0[rows, :], lead[...], across)

    @pl.when(step == pl.num_programs(0) - 1)
    def _():
        lane = lax.broadcasted_iota(jnp.int32, (width, 128), 1)
        one = jnp.sum(sum_one[...], axis=1, keepdims=True)
        sum_lead[...] = jnp.where(lane == 5, one, sum_lead[...])
        two = jnp.sum(sum_two[...], axis=1, keepdims=True)
        sum_lead[:basis, :] = jnp.where(lane[:basis] == 6, two, sum_lead[:basis, :])
        core = core_ref[0]
        half = width // 2
        for target, start in ((other_ref, (1 - core) * half), (mine_ref, core * half)):
            rows = pl.ds(pl.multiple_of(start, half), half)
            at = 0
            for total in (sum_mid, sum_out, sum_lead):
                target[:, at : at + total.shape[1]] = total[rows, :].astype(target.dtype)
                at += total.shape[1]


def trunk_back(core, delta_2, low, high, points, out, mid):
    width, half = low.shape
    basis = delta_2.shape[0]
    steps = half // TILE
    columns = width + basis + 128

    def whole(values):
        return pl.BlockSpec(values.shape, lambda i, c: (0, 0), pipeline_mode=pl.Buffered(1))

    def part(rows):
        return pl.BlockSpec((rows, TILE), lambda i, c: (0, i))

    product = 2 * half * (2 * width * basis + 2 * width * width + width * 128)
    return pl.pallas_call(
        trunk_back_kernel,
        grid_spec=pltpu.PrefetchScalarGridSpec(
            num_scalar_prefetch=1,
            grid=(steps,),
            in_specs=[
                part(basis),
                part(width),
                part(width),
                pl.BlockSpec((points.shape[0], TILE), lambda i, c: (0, c[0] * steps + i)),
                whole(out),
                whole(mid),
            ],
            out_specs=[pl.BlockSpec((width // 2, columns), lambda i, c: (0, 0))] * 2,
            scratch_shapes=[
                pltpu.VMEM((width, width), F32),
                pltpu.VMEM((width, basis), F32),
                pltpu.VMEM((width, 128), F32),
                pltpu.VMEM((width, 128), F32),
                pltpu.VMEM((basis, 128), F32),
                pltpu.VMEM((width, TILE), BF),
                pltpu.VMEM((width, TILE), BF),
                pltpu.VMEM((128, TILE), BF),
            ],
        ),
        out_shape=[
            jax.ShapeDtypeStruct((width // 2, columns), BF),
            jax.ShapeDtypeStruct((width // 2, columns), BF),
        ],
        compiler_params=pltpu.CompilerParams(
            dimension_semantics=("arbitrary",), vmem_limit_bytes=ROOM * 1024 * 1024
        ),
        cost_estimate=pl.CostEstimate(
            flops=product, bytes_accessed=24 * 1024 * 1024, transcendentals=0
        ),
        name="trunk_back",
    )(core.reshape(1), delta_2, low, high, points, out, mid)


def call(kernel, grid, ins, outs, shapes, scratch, flops, moved, limit=ROOM):
    return pl.pallas_call(
        kernel,
        grid_spec=pltpu.PrefetchScalarGridSpec(
            num_scalar_prefetch=1, grid=(grid,), in_specs=ins, out_specs=outs, scratch_shapes=scratch
        ),
        out_shape=shapes,
        compiler_params=pltpu.CompilerParams(
            dimension_semantics=("arbitrary",), vmem_limit_bytes=limit * 1024 * 1024
        ),
        cost_estimate=pl.CostEstimate(flops=flops, bytes_accessed=moved, transcendentals=0),
    )


def send_kernel(core_ref, field_ref, sent_ref):
    sent_ref[...] = field_ref[...]


def take_other_half(core, cotangent):
    rows, columns = cotangent.shape
    tile = 256
    return call(
        send_kernel,
        rows // tile,
        [pl.BlockSpec((tile, columns // 2), lambda i, c: (i, 1 - c[0]))],
        pl.BlockSpec((tile, columns // 2), lambda i, c: (i, 0)),
        jax.ShapeDtypeStruct((rows, columns // 2), BF),
        [],
        0,
        2 * rows * columns,
    )(core.reshape(1), cotangent)


def head_kernel(
    factor,
    core_ref,
    kept_ref,
    theirs_ref,
    high_ref,
    coeffs_ref,
    out_ref,
    bias_ref,
    delta_ref,
    coef_ref,
    basis_ref,
    flipped,
    column,
    mine,
    other,
):
    step = pl.program_id(0)
    scans = kept_ref.shape[0]
    basis = basis_ref.shape[0]

    @pl.when(step == 0)
    def _():
        flipped[...] = out_ref[...].T
        column[...] = jnp.broadcast_to(bias_ref[...], (128, basis)).T
        mine[...] = jnp.zeros_like(mine)
        other[...] = jnp.zeros_like(other)

    for at in range(0, basis, CHUNK):
        rows = slice(at, at + CHUNK)
        summed = dot(flipped[rows, :], high_ref[...], ((1,), (0,))) + column[rows, :1]
        basis_ref[rows, :] = jnp.tanh(summed).astype(BF)
    for at in range(0, basis, CHUNK):
        rows = slice(at, at + CHUNK)
        mine[:, rows] += dot(kept_ref[...], basis_ref[rows, :], ((1,), (1,)))
        other[:, rows] += dot(theirs_ref[...], basis_ref[rows, :], ((1,), (1,)))
        pulled = dot(coeffs_ref[rows, :scans], kept_ref[...], ((1,), (0,)))
        pulled += dot(coeffs_ref[rows, scans:], theirs_ref[...], ((1,), (0,)))
        delta_ref[rows, :] = (factor * pulled * slope(basis_ref[rows, :])).astype(BF)

    @pl.when(step == pl.num_programs(0) - 1)
    def _():
        core = core_ref[0]
        coef_ref[pl.ds(pl.multiple_of(core * scans, scans), scans), :] = mine[...].astype(BF)
        coef_ref[pl.ds(pl.multiple_of((1 - core) * scans, scans), scans), :] = other[...].astype(BF)


def trunk_head(core, cotangent, theirs, high, coeffs, out, bias, factor):
    width, half = high.shape
    basis = out.shape[1]
    scans = cotangent.shape[0]
    steps = half // TILE
    return call(
        functools.partial(head_kernel, factor),
        steps,
        [
            pl.BlockSpec((scans, TILE), lambda i, c: (0, c[0] * steps + i)),
            pl.BlockSpec((scans, TILE), lambda i, c: (0, i)),
            pl.BlockSpec((width, TILE), lambda i, c: (0, i)),
            pl.BlockSpec((basis, 2 * scans), lambda i, c: (0, 0)),
            pl.BlockSpec((width, basis), lambda i, c: (0, 0)),
            pl.BlockSpec((1, basis), lambda i, c: (0, 0)),
        ],
        [
            pl.BlockSpec((basis, TILE), lambda i, c: (0, i)),
            pl.BlockSpec((2 * scans, basis), lambda i, c: (0, 0)),
        ],
        [
            jax.ShapeDtypeStruct((basis, half), BF),
            jax.ShapeDtypeStruct((2 * scans, basis), BF),
        ],
        [
            pltpu.VMEM((basis, TILE), BF),
            pltpu.VMEM((basis, width), BF),
            pltpu.VMEM((basis, 128), F32),
            pltpu.VMEM((scans, basis), F32),
            pltpu.VMEM((scans, basis), F32),
        ],
        2 * half * basis * (width + 4 * scans),
        15 * 1024 * 1024,
    )(core.reshape(1), cotangent, theirs, high, coeffs, out, bias.reshape(1, basis))


def load_kernel(factor, core_ref, parts_ref, mine_ref, swapped_ref, load_ref, coef):
    columns = mine_ref.shape[1]
    basis = parts_ref.shape[1]

    @pl.when(pl.program_id(0) == 0)
    def _():
        total = jnp.zeros((16, basis), F32)
        for at in range(0, parts_ref.shape[0], 16):
            total += parts_ref[at : at + 16, :].astype(F32)
        total = total * factor
        flat = jnp.concatenate([total[:8], total[8:]], axis=1)
        coef[...] = jnp.concatenate([flat, flat], axis=0).astype(BF)

    load_ref[:, :columns] = (mine_ref[...].astype(F32) + swapped_ref[...].astype(F32)).astype(BF)
    for at in range(0, load_ref.shape[0], 16):
        load_ref[at : at + 16, columns:] = coef[...]


def pack_load(core, parts, mine, swapped, factor):
    rows, columns = mine.shape
    basis = parts.shape[1]
    tile = 256
    return call(
        functools.partial(load_kernel, factor),
        rows // tile,
        [
            pl.BlockSpec(parts.shape, lambda i, c: (0, 0)),
            pl.BlockSpec((tile, columns), lambda i, c: (i, 0)),
            pl.BlockSpec((tile, columns), lambda i, c: (i, 0)),
        ],
        pl.BlockSpec((tile, columns + 2 * basis), lambda i, c: (i, 0)),
        jax.ShapeDtypeStruct((rows, columns + 2 * basis), BF),
        [pltpu.VMEM((16, 2 * basis), BF)],
        0,
        9 * 1024 * 1024,
    )(core.reshape(1), parts, mine, swapped)


def total_kernel(core_ref, got_ref, wide_ref, coef_ref):
    rows, columns = wide_ref.shape
    total = jnp.zeros((16, columns), F32)
    for at in range(0, rows, 16):
        total += got_ref[at : at + 16, :columns].astype(F32)
        coef_ref[at : at + 16, :] = got_ref[at : at + 16, columns:]
    total = total[:8] + total[8:]
    both = jnp.concatenate([total, total], axis=0).astype(BF)
    for at in range(0, rows, 16):
        wide_ref[at : at + 16, :] = both


def sum_spread(core, got, columns):
    rows, wide = got.shape
    return call(
        total_kernel,
        1,
        [pl.BlockSpec((rows, wide), lambda i, c: (0, 0))],
        [
            pl.BlockSpec((rows, columns), lambda i, c: (0, 0)),
            pl.BlockSpec((rows, wide - columns), lambda i, c: (0, 0)),
        ],
        [
            jax.ShapeDtypeStruct((rows, columns), BF),
            jax.ShapeDtypeStruct((rows, wide - columns), BF),
        ],
        [],
        0,
        2 * rows * wide * 2,
    )(core.reshape(1), got)


def unpack_kernel(core_ref, own_ref, *refs):
    mid_ref, out_ref, in_ref, zero_ref, one_ref, two_ref = refs[-6:]
    width, basis = mid_ref.shape[1], out_ref.shape[1]
    mid_ref[...] = own_ref[:, :width].astype(F32)
    out_ref[...] = own_ref[:, width : width + basis].astype(F32)
    small = own_ref[:, width + basis :].astype(F32).T
    in_ref[...] = small[:4]
    zero_ref[...] = small[4:5]
    one_ref[...] = small[5:6]
    kept = refs[5][...] if len(refs) > 6 else small[6:7]
    two_ref[...] = jnp.where(core_ref[0] == 0, small[6:7], kept)


def unpack(side, own, width, basis, earlier=()):
    rows, columns = own.shape
    tile = 256
    steps = rows // tile

    def row(i, c):
        return (c[0] * steps + i, 0)

    def lane(i, c):
        return (0, c[0] * steps + i)

    return pl.pallas_call(
        unpack_kernel,
        grid_spec=pltpu.PrefetchScalarGridSpec(
            num_scalar_prefetch=1,
            grid=(steps,),
            in_specs=[pl.BlockSpec((tile, columns), lambda i, c: (i, 0))]
            + [pl.BlockSpec(memory_space=pl.ANY)] * (len(earlier) - 1)
            + [pl.BlockSpec((1, tile), lambda i, c: (0, i))] * (len(earlier) > 0),
            out_specs=[
                pl.BlockSpec((tile, width), row),
                pl.BlockSpec((tile, basis), row),
                pl.BlockSpec((4, tile), lane),
                pl.BlockSpec((1, tile), lane),
                pl.BlockSpec((1, tile), lane),
                pl.BlockSpec((1, tile), lambda i, c: (0, i)),
            ],
        ),
        out_shape=[
            jax.ShapeDtypeStruct((width, width), F32),
            jax.ShapeDtypeStruct((width, basis), F32),
            jax.ShapeDtypeStruct((4, width), F32),
            jax.ShapeDtypeStruct((1, width), F32),
            jax.ShapeDtypeStruct((1, width), F32),
            jax.ShapeDtypeStruct((1, basis), F32),
        ],
        input_output_aliases={2 + at: at for at in range(len(earlier))},
        compiler_params=pltpu.CompilerParams(
            dimension_semantics=("arbitrary",), vmem_limit_bytes=16 * 1024 * 1024
        ),
        cost_estimate=pl.CostEstimate(
            flops=0, bytes_accessed=5 * 1024 * 1024, transcendentals=0
        ),
    )(side.reshape(1), own, *earlier)


def on_device(
    cotangent,
    scan_paths,
    query_points,
    branch_in,
    branch_in_bias,
    branch_out,
    branch_out_bias,
    trunk_in,
    trunk_in_bias,
    trunk_mid,
    trunk_mid_bias,
    trunk_out,
    trunk_out_bias,
):
    core = lax.axis_index("core")
    scan_rows, point_cols = cotangent.shape
    half = point_cols // 2
    chips = lax.axis_size(CHIPS)
    pts = lax.axis_size(PTS)
    factor = 1.0 / math.sqrt(scan_rows * 4 * point_cols * pts)
    width = trunk_in.shape[1]
    basis = trunk_out.shape[1]

    theirs = swap(take_other_half(core, cotangent), "core")
    pair_paths = swap(scan_paths, "core")
    zl = lax.axis_index("zl")
    points = lax.dynamic_slice_in_dim(query_points, core * half, half, 1)

    trunk_0 = dot(trunk_in, points, ((0,), (0,))) + trunk_in_bias[:, None]
    trunk_0 = jnp.tanh(trunk_0).astype(BF)
    trunk_1 = dot(trunk_mid[0], trunk_0, ((0,), (0,))) + trunk_mid_bias[0][:, None]
    trunk_1 = jnp.tanh(trunk_1).astype(BF)
    local_paths = jnp.concatenate([scan_paths, pair_paths], axis=0)
    side_paths = swap(local_paths, "zl")

    hidden_local = tanh_layer(local_paths, branch_in, branch_in_bias)
    coeffs = dot(branch_out, hidden_local, ((0,), (1,))) + branch_out_bias[:, None]
    coeffs = coeffs.astype(BF)

    delta_2, coef_part = trunk_head(
        core, cotangent, theirs, trunk_1, coeffs, trunk_out, trunk_out_bias, factor
    )
    coef_parts = exchange(coef_part, ("core",) + PTS)

    other, mine = trunk_back(
        core, delta_2, trunk_0, trunk_1, query_points, trunk_out, trunk_mid[0]
    )
    coef_parts, side_paths, other = lax.optimization_barrier((coef_parts, side_paths, other))

    columns = mine.shape[1]
    load = pack_load(core, coef_parts, mine, swap(other, "core"), factor)
    got = exchange(load, CHIPS)
    local = local_paths.reshape(2, scan_rows, -1)
    side = side_paths.reshape(2, scan_rows, -1)
    paths = jnp.where(
        zl == 0, jnp.stack([local, side], axis=1), jnp.stack([side, local], axis=1)
    ).reshape(4 * scan_rows, -1)
    hidden = tanh_layer(paths, branch_in, branch_in_bias)
    got, hidden = lax.optimization_barrier((got, hidden))
    wide, coef_own = sum_spread(core, got, columns)
    spread = exchange(wide, CHIPS)

    coef_all = jnp.stack([coef_own, swap(coef_own, "core")])
    rows = coef_own.shape[0] // chips
    coef_all = coef_all.reshape(2, chips, rows, 2, basis).transpose(0, 1, 3, 2, 4)
    coef_all = coef_all.reshape(4 * scan_rows, basis)
    grad_branch_out = rows_rows(hidden, coef_all)
    grad_branch_out_bias = jnp.sum(coef_all.astype(F32), axis=0)
    branch_delta = (dot(coef_all, branch_out, ((1,), (1,))) * slope(hidden)).astype(BF)
    grad_branch_in = rows_rows(paths, branch_delta)
    grad_branch_in_bias = jnp.sum(branch_delta.astype(F32), axis=0)

    spread, grad_branch_out, grad_branch_in, grad_branch_out_bias = lax.optimization_barrier(
        (spread, grad_branch_out, grad_branch_in, grad_branch_out_bias)
    )
    spread_theirs = swap(spread, "core")
    first = unpack(core, spread, width, basis)
    grad_mid, grad_out, grad_in, bias_0, bias_1, bias_2 = unpack(
        1 - core, spread_theirs, width, basis, first
    )
    return (
        grad_branch_in,
        grad_branch_in_bias,
        grad_branch_out,
        grad_branch_out_bias,
        grad_in,
        bias_0[0],
        grad_mid[None],
        bias_1,
        grad_out,
        bias_2[0],
    )


def solution(mesh):
    fine = Mesh(mesh.devices.reshape(2, 2, 4, 4, 2), ALL)
    scan, pts = ("zl", "core"), PTS
    placed = (P(scan, pts), P(scan, None), P(None, pts)) + (P(),) * 10
    return jax.shard_map(
        on_device, mesh=fine, in_specs=placed, out_specs=(P(),) * 10, check_vma=False
    )
```

```python
import functools
import math

import jax
import jax.numpy as jnp
from jax import lax
from jax.experimental import pallas as pl
from jax.experimental.pallas import tpu as pltpu
from jax.sharding import Mesh, PartitionSpec as P

ALL = ("zl", "core", "y", "x", "zh")
CHIPS = ("zl", "y", "x", "zh")
PTS = ("y", "x", "zh")
BF = jnp.bfloat16
F32 = jnp.float32


def dot(left, right, dims):
    return lax.dot_general(left, right, (dims, ((), ())), preferred_element_type=F32)


def rows_rows(left, right):
    return dot(left, right, ((0,), (0,)))


def swap(values, axis):
    return lax.ppermute(values, axis, [(0, 1), (1, 0)])


def exchange(values, axes):
    return lax.all_to_all(values, axes, split_axis=0, concat_axis=0, tiled=True)


def tanh_layer(inputs, weights, offsets):
    return jnp.tanh(dot(inputs, weights, ((1,), (0,))) + offsets).astype(BF)


def slope(values):
    wide = values.astype(F32)
    return 1.0 - wide * wide


TILE = 512
ROOM = 60
CHUNK = 256


def trunk_back_kernel(
    core_ref,
    delta_2,
    low_ref,
    high_ref,
    points_ref,
    out_ref,
    mid_ref,
    other_ref,
    delta_1,
    tail_ref,
    sum_mid,
    sum_out,
    sum_lead,
    sum_one,
    sum_two,
    delta_0,
    lead,
):
    step = pl.program_id(0)
    width, tile = low_ref.shape
    half = width // 2
    basis = delta_2.shape[0]
    core = core_ref[0]

    @pl.when(step == 0)
    def _():
        for total in (sum_mid, sum_out, sum_lead, sum_one, sum_two):
            total[...] = jnp.zeros_like(total)
        lead[...] = jnp.zeros_like(lead)

    ones, blank = jnp.ones((1, tile), F32), jnp.zeros((11, tile), F32)
    lead[:16, :] = jnp.concatenate([points_ref[...].astype(F32), ones, blank], axis=0).astype(BF)

    def lanes(values):
        return functools.reduce(
            jnp.add, [values[:, at : at + 128] for at in range(0, tile, 128)]
        )

    plain, across = ((1,), (0,)), ((1,), (1,))
    sum_two[...] += lanes(delta_2[...].astype(F32))
    for at in range(0, width, CHUNK):
        rows = slice(at, at + CHUNK)
        delta = dot(out_ref[rows, :], delta_2[...], plain) * slope(high_ref[rows, :])
        sum_one[rows, :] += lanes(delta)
        delta_1[rows, :] = delta.astype(BF)
    for at in range(0, width, CHUNK):
        rows = slice(at, at + CHUNK)
        delta = dot(mid_ref[rows, :], delta_1[...], plain) * slope(low_ref[rows, :])
        delta_0[rows, :] = delta.astype(BF)
    for at in range(0, width, CHUNK):
        rows = slice(at, at + CHUNK)
        sum_lead[rows, :] += dot(delta_0[rows, :], lead[...], across)
    for at in range(0, half, CHUNK):
        rows = slice(at, at + CHUNK)
        read = pl.ds(pl.multiple_of((1 - core) * half + at, CHUNK), CHUNK)
        sum_out[rows, :] += dot(high_ref[read, :], delta_2[...], across)
        sum_mid[rows, :] += dot(low_ref[read, :], delta_1[...], across)

    @pl.when(step == pl.num_programs(0) - 1)
    def _():
        lane = lax.broadcasted_iota(jnp.int32, (width, 128), 1)
        one = jnp.sum(sum_one[...], axis=1, keepdims=True)
        sum_lead[...] = jnp.where(lane == 5, one, sum_lead[...])
        two = jnp.sum(sum_two[...], axis=1, keepdims=True)
        sum_lead[:basis, :] = jnp.where(lane[:basis] == 6, two, sum_lead[:basis, :])
        theirs = pl.ds(pl.multiple_of((1 - core) * half, half), half)
        other_ref[:, :width] = sum_mid[...].astype(BF)
        other_ref[:, width : width + basis] = sum_out[...].astype(BF)
        other_ref[:, width + basis :] = sum_lead[theirs, :].astype(BF)
        tail_ref[...] = sum_lead[pl.ds(pl.multiple_of(core * half, half), half), :]


def trunk_back(core, delta_2, low, high, points, out, mid):
    width, half = low.shape
    basis = delta_2.shape[0]
    steps = half // TILE
    columns = width + basis + 128

    def whole(values):
        return pl.BlockSpec(values.shape, lambda i, c: (0, 0), pipeline_mode=pl.Buffered(1))

    def part(rows):
        return pl.BlockSpec((rows, TILE), lambda i, c: (0, i))

    return call(
        trunk_back_kernel,
        steps,
        [
            part(basis),
            part(width),
            part(width),
            pl.BlockSpec((points.shape[0], TILE), lambda i, c: (0, c[0] * steps + i)),
            whole(out),
            whole(mid),
        ],
        [
            pl.BlockSpec((width // 2, columns), lambda i, c: (0, 0)),
            part(width),
            pl.BlockSpec((width // 2, 128), lambda i, c: (0, 0)),
        ],
        [
            jax.ShapeDtypeStruct((width // 2, columns), BF),
            jax.ShapeDtypeStruct((width, half), BF),
            jax.ShapeDtypeStruct((width // 2, 128), F32),
        ],
        [
            pltpu.VMEM((width // 2, width), F32),
            pltpu.VMEM((width // 2, basis), F32),
            pltpu.VMEM((width, 128), F32),
            pltpu.VMEM((width, 128), F32),
            pltpu.VMEM((basis, 128), F32),
            pltpu.VMEM((width, TILE), BF),
            pltpu.VMEM((128, TILE), BF),
        ],
        half * width * (3 * basis + 3 * width + 256),
        20 * 1024 * 1024,
    )(core.reshape(1), delta_2, low, high, points, out, mid)


def own_grads_kernel(
    core_ref, delta_2, delta_1, low_ref, high_ref, tail_ref, mine_ref, sum_mid, sum_out
):
    step = pl.program_id(0)
    width, basis = sum_mid.shape[1], sum_out.shape[1]

    @pl.when(step == 0)
    def _():
        sum_mid[...] = jnp.zeros_like(sum_mid)
        sum_out[...] = jnp.zeros_like(sum_out)

    for at in range(0, low_ref.shape[0], CHUNK):
        rows = slice(at, at + CHUNK)
        sum_out[rows, :] += dot(high_ref[rows, :], delta_2[...], ((1,), (1,)))
        sum_mid[rows, :] += dot(low_ref[rows, :], delta_1[...], ((1,), (1,)))

    @pl.when(step == pl.num_programs(0) - 1)
    def _():
        mine_ref[:, :width] = sum_mid[...].astype(BF)
        mine_ref[:, width : width + basis] = sum_out[...].astype(BF)
        mine_ref[:, width + basis :] = tail_ref[...].astype(BF)


def own_grads(core, delta_2, delta_1, low, high, tail):
    width, points = low.shape
    half, basis = width // 2, delta_2.shape[0]
    columns = width + basis + 128

    def part(rows):
        return pl.BlockSpec((rows, TILE), lambda i, c: (0, i))

    own = pl.BlockSpec((half, TILE), lambda i, c: (c[0], i))
    return call(
        own_grads_kernel,
        points // TILE,
        [part(basis), part(width), own, own, pl.BlockSpec(tail.shape, lambda i, c: (0, 0))],
        pl.BlockSpec((half, columns), lambda i, c: (0, 0)),
        jax.ShapeDtypeStruct((half, columns), BF),
        [pltpu.VMEM((half, width), F32), pltpu.VMEM((half, basis), F32)],
        2 * half * points * (width + basis),
        12 * 1024 * 1024,
    )(core.reshape(1), delta_2, delta_1, low, high, tail)


def call(kernel, grid, ins, outs, shapes, scratch, flops, moved, limit=ROOM):
    return pl.pallas_call(
        kernel,
        grid_spec=pltpu.PrefetchScalarGridSpec(
            num_scalar_prefetch=1, grid=(grid,), in_specs=ins, out_specs=outs, scratch_shapes=scratch
        ),
        out_shape=shapes,
        compiler_params=pltpu.CompilerParams(
            dimension_semantics=("arbitrary",), vmem_limit_bytes=limit * 1024 * 1024
        ),
        cost_estimate=pl.CostEstimate(flops=flops, bytes_accessed=moved, transcendentals=0),
    )


def send_kernel(core_ref, field_ref, sent_ref):
    sent_ref[...] = field_ref[...]


def take_other_half(core, cotangent):
    rows, columns = cotangent.shape
    tile = 256
    return call(
        send_kernel,
        rows // tile,
        [pl.BlockSpec((tile, columns // 2), lambda i, c: (i, 1 - c[0]))],
        pl.BlockSpec((tile, columns // 2), lambda i, c: (i, 0)),
        jax.ShapeDtypeStruct((rows, columns // 2), BF),
        [],
        0,
        2 * rows * columns,
    )(core.reshape(1), cotangent)


def head_kernel(
    factor,
    core_ref,
    kept_ref,
    theirs_ref,
    high_ref,
    coeffs_ref,
    out_ref,
    bias_ref,
    delta_ref,
    coef_ref,
    basis_ref,
    flipped,
    column,
    mine,
    other,
):
    step = pl.program_id(0)
    scans = kept_ref.shape[0]
    basis = basis_ref.shape[0]

    @pl.when(step == 0)
    def _():
        flipped[...] = out_ref[...].T
        column[...] = jnp.broadcast_to(bias_ref[...], (128, basis)).T
        mine[...] = jnp.zeros_like(mine)
        other[...] = jnp.zeros_like(other)

    for at in range(0, basis, CHUNK):
        rows = slice(at, at + CHUNK)
        summed = dot(flipped[rows, :], high_ref[...], ((1,), (0,))) + column[rows, :1]
        basis_ref[rows, :] = jnp.tanh(summed).astype(BF)
    for at in range(0, basis, CHUNK):
        rows = slice(at, at + CHUNK)
        mine[:, rows] += dot(kept_ref[...], basis_ref[rows, :], ((1,), (1,)))
        other[:, rows] += dot(theirs_ref[...], basis_ref[rows, :], ((1,), (1,)))
        pulled = dot(coeffs_ref[rows, :scans], kept_ref[...], ((1,), (0,)))
        pulled += dot(coeffs_ref[rows, scans:], theirs_ref[...], ((1,), (0,)))
        delta_ref[rows, :] = (factor * pulled * slope(basis_ref[rows, :])).astype(BF)

    @pl.when(step == pl.num_programs(0) - 1)
    def _():
        core = core_ref[0]
        coef_ref[pl.ds(pl.multiple_of(core * scans, scans), scans), :] = mine[...].astype(BF)
        coef_ref[pl.ds(pl.multiple_of((1 - core) * scans, scans), scans), :] = other[...].astype(BF)


def trunk_head(core, cotangent, theirs, high, coeffs, out, bias, factor):
    width, half = high.shape
    basis = out.shape[1]
    scans = cotangent.shape[0]
    steps = half // TILE
    return call(
        functools.partial(head_kernel, factor),
        steps,
        [
            pl.BlockSpec((scans, TILE), lambda i, c: (0, c[0] * steps + i)),
            pl.BlockSpec((scans, TILE), lambda i, c: (0, i)),
            pl.BlockSpec((width, TILE), lambda i, c: (0, i)),
            pl.BlockSpec((basis, 2 * scans), lambda i, c: (0, 0)),
            pl.BlockSpec((width, basis), lambda i, c: (0, 0)),
            pl.BlockSpec((1, basis), lambda i, c: (0, 0)),
        ],
        [
            pl.BlockSpec((basis, TILE), lambda i, c: (0, i)),
            pl.BlockSpec((2 * scans, basis), lambda i, c: (0, 0)),
        ],
        [
            jax.ShapeDtypeStruct((basis, half), BF),
            jax.ShapeDtypeStruct((2 * scans, basis), BF),
        ],
        [
            pltpu.VMEM((basis, TILE), BF),
            pltpu.VMEM((basis, width), BF),
            pltpu.VMEM((basis, 128), F32),
            pltpu.VMEM((scans, basis), F32),
            pltpu.VMEM((scans, basis), F32),
        ],
        2 * half * basis * (width + 4 * scans),
        15 * 1024 * 1024,
    )(core.reshape(1), cotangent, theirs, high, coeffs, out, bias.reshape(1, basis))


def load_kernel(factor, core_ref, parts_ref, mine_ref, swapped_ref, load_ref, coef):
    columns = mine_ref.shape[1]
    basis = parts_ref.shape[1]

    @pl.when(pl.program_id(0) == 0)
    def _():
        total = jnp.zeros((16, basis), F32)
        for at in range(0, parts_ref.shape[0], 16):
            total += parts_ref[at : at + 16, :].astype(F32)
        total = total * factor
        flat = jnp.concatenate([total[:8], total[8:]], axis=1)
        coef[...] = jnp.concatenate([flat, flat], axis=0).astype(BF)

    load_ref[:, :columns] = (mine_ref[...].astype(F32) + swapped_ref[...].astype(F32)).astype(BF)
    for at in range(0, load_ref.shape[0], 16):
        load_ref[at : at + 16, columns:] = coef[...]


def pack_load(core, parts, mine, swapped, factor):
    rows, columns = mine.shape
    basis = parts.shape[1]
    tile = 256
    return call(
        functools.partial(load_kernel, factor),
        rows // tile,
        [
            pl.BlockSpec(parts.shape, lambda i, c: (0, 0)),
            pl.BlockSpec((tile, columns), lambda i, c: (i, 0)),
            pl.BlockSpec((tile, columns), lambda i, c: (i, 0)),
        ],
        pl.BlockSpec((tile, columns + 2 * basis), lambda i, c: (i, 0)),
        jax.ShapeDtypeStruct((rows, columns + 2 * basis), BF),
        [pltpu.VMEM((16, 2 * basis), BF)],
        0,
        9 * 1024 * 1024,
    )(core.reshape(1), parts, mine, swapped)


def total_kernel(core_ref, got_ref, wide_ref, coef_ref):
    rows, columns = wide_ref.shape
    total = jnp.zeros((16, columns), F32)
    for at in range(0, rows, 16):
        total += got_ref[at : at + 16, :columns].astype(F32)
        coef_ref[at : at + 16, :] = got_ref[at : at + 16, columns:]
    total = total[:8] + total[8:]
    both = jnp.concatenate([total, total], axis=0).astype(BF)
    for at in range(0, rows, 16):
        wide_ref[at : at + 16, :] = both


def sum_spread(core, got, columns):
    rows, wide = got.shape
    return call(
        total_kernel,
        1,
        [pl.BlockSpec((rows, wide), lambda i, c: (0, 0))],
        [
            pl.BlockSpec((rows, columns), lambda i, c: (0, 0)),
            pl.BlockSpec((rows, wide - columns), lambda i, c: (0, 0)),
        ],
        [
            jax.ShapeDtypeStruct((rows, columns), BF),
            jax.ShapeDtypeStruct((rows, wide - columns), BF),
        ],
        [],
        0,
        2 * rows * wide * 2,
    )(core.reshape(1), got)


def unpack_kernel(core_ref, own_ref, *refs):
    mid_ref, out_ref, in_ref, zero_ref, one_ref, two_ref = refs[-6:]
    width, basis = mid_ref.shape[1], out_ref.shape[1]
    mid_ref[...] = own_ref[:, :width].astype(F32)
    out_ref[...] = own_ref[:, width : width + basis].astype(F32)
    small = own_ref[:, width + basis :].astype(F32).T
    in_ref[...] = small[:4]
    zero_ref[...] = small[4:5]
    one_ref[...] = small[5:6]
    kept = refs[5][...] if len(refs) > 6 else small[6:7]
    two_ref[...] = jnp.where(core_ref[0] == 0, small[6:7], kept)


def unpack(side, own, width, basis, earlier=()):
    rows, columns = own.shape
    tile = 256
    steps = rows // tile

    def row(i, c):
        return (c[0] * steps + i, 0)

    def lane(i, c):
        return (0, c[0] * steps + i)

    return pl.pallas_call(
        unpack_kernel,
        grid_spec=pltpu.PrefetchScalarGridSpec(
            num_scalar_prefetch=1,
            grid=(steps,),
            in_specs=[pl.BlockSpec((tile, columns), lambda i, c: (i, 0))]
            + [pl.BlockSpec(memory_space=pl.ANY)] * (len(earlier) - 1)
            + [pl.BlockSpec((1, tile), lambda i, c: (0, i))] * (len(earlier) > 0),
            out_specs=[
                pl.BlockSpec((tile, width), row),
                pl.BlockSpec((tile, basis), row),
                pl.BlockSpec((4, tile), lane),
                pl.BlockSpec((1, tile), lane),
                pl.BlockSpec((1, tile), lane),
                pl.BlockSpec((1, tile), lambda i, c: (0, i)),
            ],
        ),
        out_shape=[
            jax.ShapeDtypeStruct((width, width), F32),
            jax.ShapeDtypeStruct((width, basis), F32),
            jax.ShapeDtypeStruct((4, width), F32),
            jax.ShapeDtypeStruct((1, width), F32),
            jax.ShapeDtypeStruct((1, width), F32),
            jax.ShapeDtypeStruct((1, basis), F32),
        ],
        input_output_aliases={2 + at: at for at in range(len(earlier))},
        compiler_params=pltpu.CompilerParams(
            dimension_semantics=("arbitrary",), vmem_limit_bytes=16 * 1024 * 1024
        ),
        cost_estimate=pl.CostEstimate(
            flops=0, bytes_accessed=5 * 1024 * 1024, transcendentals=0
        ),
    )(side.reshape(1), own, *earlier)


def on_device(
    cotangent,
    scan_paths,
    query_points,
    branch_in,
    branch_in_bias,
    branch_out,
    branch_out_bias,
    trunk_in,
    trunk_in_bias,
    trunk_mid,
    trunk_mid_bias,
    trunk_out,
    trunk_out_bias,
):
    core = lax.axis_index("core")
    scan_rows, point_cols = cotangent.shape
    half = point_cols // 2
    chips = lax.axis_size(CHIPS)
    pts = lax.axis_size(PTS)
    factor = 1.0 / math.sqrt(scan_rows * 4 * point_cols * pts)
    width = trunk_in.shape[1]
    basis = trunk_out.shape[1]

    theirs = swap(take_other_half(core, cotangent), "core")
    pair_paths = swap(scan_paths, "core")
    zl = lax.axis_index("zl")
    points = lax.dynamic_slice_in_dim(query_points, core * half, half, 1)

    trunk_0 = dot(trunk_in, points, ((0,), (0,))) + trunk_in_bias[:, None]
    trunk_0 = jnp.tanh(trunk_0).astype(BF)
    trunk_1 = dot(trunk_mid[0], trunk_0, ((0,), (0,))) + trunk_mid_bias[0][:, None]
    trunk_1 = jnp.tanh(trunk_1).astype(BF)
    local_paths = jnp.concatenate([scan_paths, pair_paths], axis=0)
    side_paths = swap(local_paths, "zl")

    hidden_local = tanh_layer(local_paths, branch_in, branch_in_bias)
    coeffs = dot(branch_out, hidden_local, ((0,), (1,))) + branch_out_bias[:, None]
    coeffs = coeffs.astype(BF)

    delta_2, coef_part = trunk_head(
        core, cotangent, theirs, trunk_1, coeffs, trunk_out, trunk_out_bias, factor
    )
    coef_parts = exchange(coef_part, ("core",) + PTS)

    other, delta_1, tail = trunk_back(
        core, delta_2, trunk_0, trunk_1, query_points, trunk_out, trunk_mid[0]
    )
    coef_parts, side_paths, other = lax.optimization_barrier((coef_parts, side_paths, other))
    swapped = swap(other, "core")
    mine = own_grads(core, delta_2, delta_1, trunk_0, trunk_1, tail)

    columns = mine.shape[1]
    load = pack_load(core, coef_parts, mine, swapped, factor)
    got = exchange(load, CHIPS)
    local = local_paths.reshape(2, scan_rows, -1)
    side = side_paths.reshape(2, scan_rows, -1)
    paths = jnp.where(
        zl == 0, jnp.stack([local, side], axis=1), jnp.stack([side, local], axis=1)
    ).reshape(4 * scan_rows, -1)
    hidden = tanh_layer(paths, branch_in, branch_in_bias)
    got, hidden = lax.optimization_barrier((got, hidden))
    wide, coef_own = sum_spread(core, got, columns)
    spread = exchange(wide, CHIPS)

    coef_all = jnp.stack([coef_own, swap(coef_own, "core")])
    rows = coef_own.shape[0] // chips
    coef_all = coef_all.reshape(2, chips, rows, 2, basis).transpose(0, 1, 3, 2, 4)
    coef_all = coef_all.reshape(4 * scan_rows, basis)
    grad_branch_out = rows_rows(hidden, coef_all)
    grad_branch_out_bias = jnp.sum(coef_all.astype(F32), axis=0)
    branch_delta = (dot(coef_all, branch_out, ((1,), (1,))) * slope(hidden)).astype(BF)
    grad_branch_in = rows_rows(paths, branch_delta)
    grad_branch_in_bias = jnp.sum(branch_delta.astype(F32), axis=0)

    spread, grad_branch_out, grad_branch_in, grad_branch_out_bias = lax.optimization_barrier(
        (spread, grad_branch_out, grad_branch_in, grad_branch_out_bias)
    )
    spread_theirs = swap(spread, "core")
    first = unpack(core, spread, width, basis)
    grad_mid, grad_out, grad_in, bias_0, bias_1, bias_2 = unpack(
        1 - core, spread_theirs, width, basis, first
    )
    return (
        grad_branch_in,
        grad_branch_in_bias,
        grad_branch_out,
        grad_branch_out_bias,
        grad_in,
        bias_0[0],
        grad_mid[None],
        bias_1,
        grad_out,
        bias_2[0],
    )


def solution(mesh):
    fine = Mesh(mesh.devices.reshape(2, 2, 4, 4, 2), ALL)
    scan, pts = ("zl", "core"), PTS
    placed = (P(scan, pts), P(scan, None), P(None, pts)) + (P(),) * 10
    return jax.shard_map(
        on_device, mesh=fine, in_specs=placed, out_specs=(P(),) * 10, check_vma=False
    )
```

```python
import functools
import math

import jax
import jax.numpy as jnp
from jax import lax
from jax.experimental import pallas as pl
from jax.experimental.pallas import tpu as pltpu
from jax.sharding import Mesh, PartitionSpec as P

ALL = ("zl", "core", "y", "x", "zh")
CHIPS = ("zl", "y", "x", "zh")
PTS = ("y", "x", "zh")
BF = jnp.bfloat16
F32 = jnp.float32


def dot(left, right, dims):
    return lax.dot_general(left, right, (dims, ((), ())), preferred_element_type=F32)


def rows_rows(left, right):
    return dot(left, right, ((0,), (0,)))


def swap(values, axis):
    return lax.ppermute(values, axis, [(0, 1), (1, 0)])


def exchange(values, axes):
    return lax.all_to_all(values, axes, split_axis=0, concat_axis=0, tiled=True)


def tanh_layer(inputs, weights, offsets):
    return jnp.tanh(dot(inputs, weights, ((1,), (0,))) + offsets).astype(BF)


def slope(values):
    wide = values.astype(F32)
    return 1.0 - wide * wide


TILE = 512
ROOM = 60
CHUNK = 256


def trunk_back_kernel(
    core_ref,
    delta_2,
    low_ref,
    high_ref,
    points_ref,
    out_ref,
    mid_ref,
    other_ref,
    mine_ref,
    sum_mid,
    sum_out,
    sum_lead,
    sum_one,
    sum_two,
    delta_1,
    delta_0,
    lead,
):
    step = pl.program_id(0)
    width, tile = low_ref.shape
    basis = delta_2.shape[0]

    @pl.when(step == 0)
    def _():
        for total in (sum_mid, sum_out, sum_lead, sum_one, sum_two):
            total[...] = jnp.zeros_like(total)
        lead[...] = jnp.zeros_like(lead)

    ones, blank = jnp.ones((1, tile), F32), jnp.zeros((11, tile), F32)
    lead[:16, :] = jnp.concatenate([points_ref[...].astype(F32), ones, blank], axis=0).astype(BF)

    def lanes(values):
        return functools.reduce(
            jnp.add, [values[:, at : at + 128] for at in range(0, tile, 128)]
        )

    plain, across = ((1,), (0,)), ((1,), (1,))
    sum_two[...] += lanes(delta_2[...].astype(F32))
    for at in range(0, width, CHUNK):
        rows = slice(at, at + CHUNK)
        delta = dot(out_ref[rows, :], delta_2[...], plain) * slope(high_ref[rows, :])
        sum_one[rows, :] += lanes(delta)
        delta_1[rows, :] = delta.astype(BF)
    for at in range(0, width, CHUNK):
        rows = slice(at, at + CHUNK)
        delta = dot(mid_ref[rows, :], delta_1[...], plain) * slope(low_ref[rows, :])
        delta_0[rows, :] = delta.astype(BF)
    for at in range(0, width, CHUNK):
        rows = slice(at, at + CHUNK)
        sum_out[rows, :] += dot(high_ref[rows, :], delta_2[...], across)
        sum_mid[rows, :] += dot(low_ref[rows, :], delta_1[...], across)
        sum_lead[rows, :] += dot(delta_0[rows, :], lead[...], across)

    @pl.when(step == pl.num_programs(0) - 1)
    def _():
        lane = lax.broadcasted_iota(jnp.int32, (width, 128), 1)
        one = jnp.sum(sum_one[...], axis=1, keepdims=True)
        sum_lead[...] = jnp.where(lane == 5, one, sum_lead[...])
        two = jnp.sum(sum_two[...], axis=1, keepdims=True)
        sum_lead[:basis, :] = jnp.where(lane[:basis] == 6, two, sum_lead[:basis, :])
        core = core_ref[0]
        half = width // 2
        for target, start in ((other_ref, (1 - core) * half), (mine_ref, core * half)):
            rows = pl.ds(pl.multiple_of(start, half), half)
            at = 0
            for total in (sum_mid, sum_out, sum_lead):
                target[:, at : at + total.shape[1]] = total[rows, :].astype(target.dtype)
                at += total.shape[1]


def trunk_back(core, delta_2, low, high, points, out, mid):
    width, half = low.shape
    basis = delta_2.shape[0]
    steps = half // TILE
    columns = width + basis + 128

    def whole(values):
        return pl.BlockSpec(values.shape, lambda i, c: (0, 0), pipeline_mode=pl.Buffered(1))

    def part(rows):
        return pl.BlockSpec((rows, TILE), lambda i, c: (0, i))

    product = 2 * half * (2 * width * basis + 2 * width * width + width * 128)
    return pl.pallas_call(
        trunk_back_kernel,
        grid_spec=pltpu.PrefetchScalarGridSpec(
            num_scalar_prefetch=1,
            grid=(steps,),
            in_specs=[
                part(basis),
                part(width),
                part(width),
                pl.BlockSpec((points.shape[0], TILE), lambda i, c: (0, c[0] * steps + i)),
                whole(out),
                whole(mid),
            ],
            out_specs=[pl.BlockSpec((width // 2, columns), lambda i, c: (0, 0))] * 2,
            scratch_shapes=[
                pltpu.VMEM((width, width), F32),
                pltpu.VMEM((width, basis), F32),
                pltpu.VMEM((width, 128), F32),
                pltpu.VMEM((width, 128), F32),
                pltpu.VMEM((basis, 128), F32),
                pltpu.VMEM((width, TILE), BF),
                pltpu.VMEM((width, TILE), BF),
                pltpu.VMEM((128, TILE), BF),
            ],
        ),
        out_shape=[
            jax.ShapeDtypeStruct((width // 2, columns), BF),
            jax.ShapeDtypeStruct((width // 2, columns), BF),
        ],
        compiler_params=pltpu.CompilerParams(
            dimension_semantics=("arbitrary",), vmem_limit_bytes=ROOM * 1024 * 1024
        ),
        cost_estimate=pl.CostEstimate(
            flops=product, bytes_accessed=24 * 1024 * 1024, transcendentals=0
        ),
        name="trunk_back",
    )(core.reshape(1), delta_2, low, high, points, out, mid)


def call(kernel, grid, ins, outs, shapes, scratch, flops, moved, limit=ROOM):
    return pl.pallas_call(
        kernel,
        grid_spec=pltpu.PrefetchScalarGridSpec(
            num_scalar_prefetch=1, grid=(grid,), in_specs=ins, out_specs=outs, scratch_shapes=scratch
        ),
        out_shape=shapes,
        compiler_params=pltpu.CompilerParams(
            dimension_semantics=("arbitrary",), vmem_limit_bytes=limit * 1024 * 1024
        ),
        cost_estimate=pl.CostEstimate(flops=flops, bytes_accessed=moved, transcendentals=0),
    )


def branch_out_kernel(core_ref, hidden_ref, coef_ref, grad_ref, bias_ref):
    grad_ref[...] = dot(hidden_ref[...], coef_ref[...], ((1,), (0,)))

    @pl.when(pl.program_id(0) == 0)
    def _():
        total = jnp.zeros((16, coef_ref.shape[1]), F32)
        for at in range(0, coef_ref.shape[0], 16):
            total += coef_ref[at : at + 16, :].astype(F32)
        bias_ref[...] = jnp.sum(total, axis=0, keepdims=True)


def branch_out_grads(core, hidden, coef):
    width, scans = hidden.shape
    basis = coef.shape[1]
    return call(
        branch_out_kernel,
        width // TILE,
        [
            pl.BlockSpec((TILE, scans), lambda i, c: (i, 0)),
            pl.BlockSpec(coef.shape, lambda i, c: (0, 0), pipeline_mode=pl.Buffered(1)),
        ],
        [
            pl.BlockSpec((TILE, basis), lambda i, c: (i, 0)),
            pl.BlockSpec((1, basis), lambda i, c: (0, 0)),
        ],
        [
            jax.ShapeDtypeStruct((width, basis), F32),
            jax.ShapeDtypeStruct((1, basis), F32),
        ],
        [],
        2 * width * scans * basis,
        14 * 1024 * 1024,
    )(core.reshape(1), hidden, coef)


def send_kernel(core_ref, field_ref, sent_ref):
    sent_ref[...] = field_ref[...]


def take_other_half(core, cotangent):
    rows, columns = cotangent.shape
    tile = 256
    return call(
        send_kernel,
        rows // tile,
        [pl.BlockSpec((tile, columns // 2), lambda i, c: (i, 1 - c[0]))],
        pl.BlockSpec((tile, columns // 2), lambda i, c: (i, 0)),
        jax.ShapeDtypeStruct((rows, columns // 2), BF),
        [],
        0,
        2 * rows * columns,
    )(core.reshape(1), cotangent)


def head_kernel(
    factor,
    core_ref,
    kept_ref,
    theirs_ref,
    high_ref,
    coeffs_ref,
    out_ref,
    bias_ref,
    delta_ref,
    coef_ref,
    basis_ref,
    flipped,
    column,
    mine,
    other,
):
    step = pl.program_id(0)
    scans = kept_ref.shape[0]
    basis = basis_ref.shape[0]

    @pl.when(step == 0)
    def _():
        flipped[...] = out_ref[...].T
        column[...] = jnp.broadcast_to(bias_ref[...], (128, basis)).T
        mine[...] = jnp.zeros_like(mine)
        other[...] = jnp.zeros_like(other)

    for at in range(0, basis, CHUNK):
        rows = slice(at, at + CHUNK)
        summed = dot(flipped[rows, :], high_ref[...], ((1,), (0,))) + column[rows, :1]
        basis_ref[rows, :] = jnp.tanh(summed).astype(BF)
    for at in range(0, basis, CHUNK):
        rows = slice(at, at + CHUNK)
        mine[:, rows] += dot(kept_ref[...], basis_ref[rows, :], ((1,), (1,)))
        other[:, rows] += dot(theirs_ref[...], basis_ref[rows, :], ((1,), (1,)))
        pulled = dot(coeffs_ref[rows, :scans], kept_ref[...], ((1,), (0,)))
        pulled += dot(coeffs_ref[rows, scans:], theirs_ref[...], ((1,), (0,)))
        delta_ref[rows, :] = (factor * pulled * slope(basis_ref[rows, :])).astype(BF)

    @pl.when(step == pl.num_programs(0) - 1)
    def _():
        core = core_ref[0]
        coef_ref[pl.ds(pl.multiple_of(core * scans, scans), scans), :] = mine[...].astype(BF)
        coef_ref[pl.ds(pl.multiple_of((1 - core) * scans, scans), scans), :] = other[...].astype(BF)


def trunk_head(core, cotangent, theirs, high, coeffs, out, bias, factor):
    width, half = high.shape
    basis = out.shape[1]
    scans = cotangent.shape[0]
    steps = half // TILE
    return call(
        functools.partial(head_kernel, factor),
        steps,
        [
            pl.BlockSpec((scans, TILE), lambda i, c: (0, c[0] * steps + i)),
            pl.BlockSpec((scans, TILE), lambda i, c: (0, i)),
            pl.BlockSpec((width, TILE), lambda i, c: (0, i)),
            pl.BlockSpec((basis, 2 * scans), lambda i, c: (0, 0)),
            pl.BlockSpec((width, basis), lambda i, c: (0, 0)),
            pl.BlockSpec((1, basis), lambda i, c: (0, 0)),
        ],
        [
            pl.BlockSpec((basis, TILE), lambda i, c: (0, i)),
            pl.BlockSpec((2 * scans, basis), lambda i, c: (0, 0)),
        ],
        [
            jax.ShapeDtypeStruct((basis, half), BF),
            jax.ShapeDtypeStruct((2 * scans, basis), BF),
        ],
        [
            pltpu.VMEM((basis, TILE), BF),
            pltpu.VMEM((basis, width), BF),
            pltpu.VMEM((basis, 128), F32),
            pltpu.VMEM((scans, basis), F32),
            pltpu.VMEM((scans, basis), F32),
        ],
        2 * half * basis * (width + 4 * scans),
        15 * 1024 * 1024,
    )(core.reshape(1), cotangent, theirs, high, coeffs, out, bias.reshape(1, basis))


def load_kernel(factor, core_ref, parts_ref, mine_ref, swapped_ref, load_ref, coef):
    columns = mine_ref.shape[1]
    basis = parts_ref.shape[1]

    @pl.when(pl.program_id(0) == 0)
    def _():
        total = jnp.zeros((16, basis), F32)
        for at in range(0, parts_ref.shape[0], 16):
            total += parts_ref[at : at + 16, :].astype(F32)
        total = total * factor
        flat = jnp.concatenate([total[:8], total[8:]], axis=1)
        coef[...] = jnp.concatenate([flat, flat], axis=0).astype(BF)

    load_ref[:, :columns] = (mine_ref[...].astype(F32) + swapped_ref[...].astype(F32)).astype(BF)
    for at in range(0, load_ref.shape[0], 16):
        load_ref[at : at + 16, columns:] = coef[...]


def pack_load(core, parts, mine, swapped, factor):
    rows, columns = mine.shape
    basis = parts.shape[1]
    tile = 256
    return call(
        functools.partial(load_kernel, factor),
        rows // tile,
        [
            pl.BlockSpec(parts.shape, lambda i, c: (0, 0)),
            pl.BlockSpec((tile, columns), lambda i, c: (i, 0)),
            pl.BlockSpec((tile, columns), lambda i, c: (i, 0)),
        ],
        pl.BlockSpec((tile, columns + 2 * basis), lambda i, c: (i, 0)),
        jax.ShapeDtypeStruct((rows, columns + 2 * basis), BF),
        [pltpu.VMEM((16, 2 * basis), BF)],
        0,
        9 * 1024 * 1024,
    )(core.reshape(1), parts, mine, swapped)


def total_kernel(core_ref, got_ref, wide_ref, coef_ref):
    rows, columns = wide_ref.shape
    total = jnp.zeros((16, columns), F32)
    for at in range(0, rows, 16):
        total += got_ref[at : at + 16, :columns].astype(F32)
        coef_ref[at : at + 16, :] = got_ref[at : at + 16, columns:]
    total = total[:8] + total[8:]
    both = jnp.concatenate([total, total], axis=0).astype(BF)
    for at in range(0, rows, 16):
        wide_ref[at : at + 16, :] = both


def sum_spread(core, got, columns):
    rows, wide = got.shape
    return call(
        total_kernel,
        1,
        [pl.BlockSpec((rows, wide), lambda i, c: (0, 0))],
        [
            pl.BlockSpec((rows, columns), lambda i, c: (0, 0)),
            pl.BlockSpec((rows, wide - columns), lambda i, c: (0, 0)),
        ],
        [
            jax.ShapeDtypeStruct((rows, columns), BF),
            jax.ShapeDtypeStruct((rows, wide - columns), BF),
        ],
        [],
        0,
        2 * rows * wide * 2,
    )(core.reshape(1), got)


def unpack_kernel(core_ref, own_ref, *refs):
    mid_ref, out_ref, in_ref, zero_ref, one_ref, two_ref = refs[-6:]
    width, basis = mid_ref.shape[1], out_ref.shape[1]
    mid_ref[...] = own_ref[:, :width].astype(F32)
    out_ref[...] = own_ref[:, width : width + basis].astype(F32)
    small = own_ref[:, width + basis :].astype(F32).T
    in_ref[...] = small[:4]
    zero_ref[...] = small[4:5]
    one_ref[...] = small[5:6]
    kept = refs[5][...] if len(refs) > 6 else small[6:7]
    two_ref[...] = jnp.where(core_ref[0] == 0, small[6:7], kept)


def unpack(side, own, width, basis, earlier=()):
    rows, columns = own.shape
    tile = 256
    steps = rows // tile

    def row(i, c):
        return (c[0] * steps + i, 0)

    def lane(i, c):
        return (0, c[0] * steps + i)

    return pl.pallas_call(
        unpack_kernel,
        grid_spec=pltpu.PrefetchScalarGridSpec(
            num_scalar_prefetch=1,
            grid=(steps,),
            in_specs=[pl.BlockSpec((tile, columns), lambda i, c: (i, 0))]
            + [pl.BlockSpec(memory_space=pl.ANY)] * (len(earlier) - 1)
            + [pl.BlockSpec((1, tile), lambda i, c: (0, i))] * (len(earlier) > 0),
            out_specs=[
                pl.BlockSpec((tile, width), row),
                pl.BlockSpec((tile, basis), row),
                pl.BlockSpec((4, tile), lane),
                pl.BlockSpec((1, tile), lane),
                pl.BlockSpec((1, tile), lane),
                pl.BlockSpec((1, tile), lambda i, c: (0, i)),
            ],
        ),
        out_shape=[
            jax.ShapeDtypeStruct((width, width), F32),
            jax.ShapeDtypeStruct((width, basis), F32),
            jax.ShapeDtypeStruct((4, width), F32),
            jax.ShapeDtypeStruct((1, width), F32),
            jax.ShapeDtypeStruct((1, width), F32),
            jax.ShapeDtypeStruct((1, basis), F32),
        ],
        input_output_aliases={2 + at: at for at in range(len(earlier))},
        compiler_params=pltpu.CompilerParams(
            dimension_semantics=("arbitrary",), vmem_limit_bytes=16 * 1024 * 1024
        ),
        cost_estimate=pl.CostEstimate(
            flops=0, bytes_accessed=5 * 1024 * 1024, transcendentals=0
        ),
    )(side.reshape(1), own, *earlier)


def on_device(
    cotangent,
    scan_paths,
    query_points,
    branch_in,
    branch_in_bias,
    branch_out,
    branch_out_bias,
    trunk_in,
    trunk_in_bias,
    trunk_mid,
    trunk_mid_bias,
    trunk_out,
    trunk_out_bias,
):
    core = lax.axis_index("core")
    scan_rows, point_cols = cotangent.shape
    half = point_cols // 2
    chips = lax.axis_size(CHIPS)
    pts = lax.axis_size(PTS)
    factor = 1.0 / math.sqrt(scan_rows * 4 * point_cols * pts)
    width = trunk_in.shape[1]
    basis = trunk_out.shape[1]

    theirs = swap(take_other_half(core, cotangent), "core")
    pair_paths = swap(scan_paths, "core")
    zl = lax.axis_index("zl")
    points = lax.dynamic_slice_in_dim(query_points, core * half, half, 1)

    trunk_0 = dot(trunk_in, points, ((0,), (0,))) + trunk_in_bias[:, None]
    trunk_0 = jnp.tanh(trunk_0).astype(BF)
    trunk_1 = dot(trunk_mid[0], trunk_0, ((0,), (0,))) + trunk_mid_bias[0][:, None]
    trunk_1 = jnp.tanh(trunk_1).astype(BF)
    local_paths = jnp.concatenate([scan_paths, pair_paths], axis=0)
    side_paths = swap(local_paths, "zl")

    hidden_local = tanh_layer(local_paths, branch_in, branch_in_bias)
    coeffs = dot(branch_out, hidden_local, ((0,), (1,))) + branch_out_bias[:, None]
    coeffs = coeffs.astype(BF)

    delta_2, coef_part = trunk_head(
        core, cotangent, theirs, trunk_1, coeffs, trunk_out, trunk_out_bias, factor
    )
    coef_parts = exchange(coef_part, ("core",) + PTS)

    other, mine = trunk_back(
        core, delta_2, trunk_0, trunk_1, query_points, trunk_out, trunk_mid[0]
    )
    coef_parts, side_paths, other = lax.optimization_barrier((coef_parts, side_paths, other))

    columns = mine.shape[1]
    load = pack_load(core, coef_parts, mine, swap(other, "core"), factor)
    got = exchange(load, CHIPS)
    local = local_paths.reshape(2, scan_rows, -1)
    side = side_paths.reshape(2, scan_rows, -1)
    paths = jnp.where(
        zl == 0, jnp.stack([local, side], axis=1), jnp.stack([side, local], axis=1)
    ).reshape(4 * scan_rows, -1)
    hidden = dot(branch_in, paths, ((0,), (1,))) + branch_in_bias[:, None]
    hidden = jnp.tanh(hidden).astype(BF)
    got, hidden = lax.optimization_barrier((got, hidden))
    wide, coef_own = sum_spread(core, got, columns)
    spread = exchange(wide, CHIPS)

    coef_all = jnp.stack([coef_own, swap(coef_own, "core")])
    rows = coef_own.shape[0] // chips
    coef_all = coef_all.reshape(2, chips, rows, 2, basis).transpose(0, 1, 3, 2, 4)
    coef_all = coef_all.reshape(4 * scan_rows, basis)
    grad_branch_out, grad_branch_out_bias = branch_out_grads(core, hidden, coef_all)
    branch_delta = (dot(branch_out, coef_all, ((1,), (1,))) * slope(hidden)).astype(BF)
    grad_branch_in = dot(paths, branch_delta, ((0,), (1,)))
    grad_branch_in_bias = jnp.sum(branch_delta.astype(F32), axis=1)

    spread, grad_branch_out, grad_branch_in, grad_branch_out_bias = lax.optimization_barrier(
        (spread, grad_branch_out, grad_branch_in, grad_branch_out_bias)
    )
    spread_theirs = swap(spread, "core")
    first = unpack(core, spread, width, basis)
    grad_mid, grad_out, grad_in, bias_0, bias_1, bias_2 = unpack(
        1 - core, spread_theirs, width, basis, first
    )
    return (
        grad_branch_in,
        grad_branch_in_bias,
        grad_branch_out,
        grad_branch_out_bias[0],
        grad_in,
        bias_0[0],
        grad_mid[None],
        bias_1,
        grad_out,
        bias_2[0],
    )


def solution(mesh):
    fine = Mesh(mesh.devices.reshape(2, 2, 4, 4, 2), ALL)
    scan, pts = ("zl", "core"), PTS
    placed = (P(scan, pts), P(scan, None), P(None, pts)) + (P(),) * 10
    return jax.shard_map(
        on_device, mesh=fine, in_specs=placed, out_specs=(P(),) * 10, check_vma=False
    )
```

```python
import functools
import math

import jax
import jax.numpy as jnp
from jax import lax
from jax.experimental import pallas as pl
from jax.experimental.pallas import tpu as pltpu
from jax.sharding import Mesh, PartitionSpec as P

ALL = ("zl", "core", "y", "x", "zh")
CHIPS = ("zl", "y", "x", "zh")
PTS = ("y", "x", "zh")
BF = jnp.bfloat16
F32 = jnp.float32


def dot(left, right, dims):
    return lax.dot_general(left, right, (dims, ((), ())), preferred_element_type=F32)


def rows_rows(left, right):
    return dot(left, right, ((0,), (0,)))


def swap(values, axis):
    return lax.ppermute(values, axis, [(0, 1), (1, 0)])


def exchange(values, axes):
    return lax.all_to_all(values, axes, split_axis=0, concat_axis=0, tiled=True)


def tanh_layer(inputs, weights, offsets):
    return jnp.tanh(dot(inputs, weights, ((1,), (0,))) + offsets).astype(BF)


def slope(values):
    wide = values.astype(F32)
    return 1.0 - wide * wide


TILE = 512
ROOM = 60
CHUNK = 256


def trunk_back_kernel(
    core_ref,
    delta_2,
    low_ref,
    high_ref,
    points_ref,
    out_ref,
    mid_ref,
    other_ref,
    mine_ref,
    sum_mid,
    sum_out,
    sum_lead,
    sum_one,
    sum_two,
    delta_1,
    delta_0,
    lead,
):
    step = pl.program_id(0)
    width, tile = low_ref.shape
    basis = delta_2.shape[0]

    @pl.when(step == 0)
    def _():
        for total in (sum_mid, sum_out, sum_lead, sum_one, sum_two):
            total[...] = jnp.zeros_like(total)
        lead[...] = jnp.zeros_like(lead)

    ones, blank = jnp.ones((1, tile), F32), jnp.zeros((11, tile), F32)
    lead[:16, :] = jnp.concatenate([points_ref[...].astype(F32), ones, blank], axis=0).astype(BF)

    def lanes(values):
        return functools.reduce(
            jnp.add, [values[:, at : at + 128] for at in range(0, tile, 128)]
        )

    plain, across = ((1,), (0,)), ((1,), (1,))
    sum_two[...] += lanes(delta_2[...].astype(F32))
    for at in range(0, width, CHUNK):
        rows = slice(at, at + CHUNK)
        delta = dot(out_ref[rows, :], delta_2[...], plain) * slope(high_ref[rows, :])
        sum_one[rows, :] += lanes(delta)
        delta_1[rows, :] = delta.astype(BF)
    for at in range(0, width, CHUNK):
        rows = slice(at, at + CHUNK)
        delta = dot(mid_ref[rows, :], delta_1[...], plain) * slope(low_ref[rows, :])
        delta_0[rows, :] = delta.astype(BF)
    for at in range(0, width, CHUNK):
        rows = slice(at, at + CHUNK)
        sum_out[rows, :] += dot(high_ref[rows, :], delta_2[...], across)
        sum_mid[rows, :] += dot(low_ref[rows, :], delta_1[...], across)
        sum_lead[rows, :] += dot(delta_0[rows, :], lead[...], across)

    @pl.when(step == pl.num_programs(0) - 1)
    def _():
        lane = lax.broadcasted_iota(jnp.int32, (width, 128), 1)
        one = jnp.sum(sum_one[...], axis=1, keepdims=True)
        sum_lead[...] = jnp.where(lane == 5, one, sum_lead[...])
        two = jnp.sum(sum_two[...], axis=1, keepdims=True)
        sum_lead[:basis, :] = jnp.where(lane[:basis] == 6, two, sum_lead[:basis, :])
        core = core_ref[0]
        half = width // 2
        for target, start in ((other_ref, (1 - core) * half), (mine_ref, core * half)):
            rows = pl.ds(pl.multiple_of(start, half), half)
            at = 0
            for total in (sum_mid, sum_out, sum_lead):
                target[:, at : at + total.shape[1]] = total[rows, :].astype(target.dtype)
                at += total.shape[1]


def trunk_back(core, delta_2, low, high, points, out, mid):
    width, half = low.shape
    basis = delta_2.shape[0]
    steps = half // TILE
    columns = width + basis + 128

    def whole(values):
        return pl.BlockSpec(values.shape, lambda i, c: (0, 0), pipeline_mode=pl.Buffered(1))

    def part(rows):
        return pl.BlockSpec((rows, TILE), lambda i, c: (0, i))

    product = 2 * half * (2 * width * basis + 2 * width * width + width * 128)
    return pl.pallas_call(
        trunk_back_kernel,
        grid_spec=pltpu.PrefetchScalarGridSpec(
            num_scalar_prefetch=1,
            grid=(steps,),
            in_specs=[
                part(basis),
                part(width),
                part(width),
                pl.BlockSpec((points.shape[0], TILE), lambda i, c: (0, c[0] * steps + i)),
                whole(out),
                whole(mid),
            ],
            out_specs=[pl.BlockSpec((width // 2, columns), lambda i, c: (0, 0))] * 2,
            scratch_shapes=[
                pltpu.VMEM((width, width), F32),
                pltpu.VMEM((width, basis), F32),
                pltpu.VMEM((width, 128), F32),
                pltpu.VMEM((width, 128), F32),
                pltpu.VMEM((basis, 128), F32),
                pltpu.VMEM((width, TILE), BF),
                pltpu.VMEM((width, TILE), BF),
                pltpu.VMEM((128, TILE), BF),
            ],
        ),
        out_shape=[
            jax.ShapeDtypeStruct((width // 2, columns), BF),
            jax.ShapeDtypeStruct((width // 2, columns), BF),
        ],
        compiler_params=pltpu.CompilerParams(
            dimension_semantics=("arbitrary",), vmem_limit_bytes=ROOM * 1024 * 1024
        ),
        cost_estimate=pl.CostEstimate(
            flops=product, bytes_accessed=24 * 1024 * 1024, transcendentals=0
        ),
        name="trunk_back",
    )(core.reshape(1), delta_2, low, high, points, out, mid)


def call(kernel, grid, ins, outs, shapes, scratch, flops, moved, limit=ROOM):
    return pl.pallas_call(
        kernel,
        grid_spec=pltpu.PrefetchScalarGridSpec(
            num_scalar_prefetch=1, grid=(grid,), in_specs=ins, out_specs=outs, scratch_shapes=scratch
        ),
        out_shape=shapes,
        compiler_params=pltpu.CompilerParams(
            dimension_semantics=("arbitrary",), vmem_limit_bytes=limit * 1024 * 1024
        ),
        cost_estimate=pl.CostEstimate(flops=flops, bytes_accessed=moved, transcendentals=0),
    )


def send_kernel(core_ref, field_ref, sent_ref):
    sent_ref[...] = field_ref[...]


def take_other_half(core, cotangent):
    rows, columns = cotangent.shape
    tile = 256
    return call(
        send_kernel,
        rows // tile,
        [pl.BlockSpec((tile, columns // 2), lambda i, c: (i, 1 - c[0]))],
        pl.BlockSpec((tile, columns // 2), lambda i, c: (i, 0)),
        jax.ShapeDtypeStruct((rows, columns // 2), BF),
        [],
        0,
        2 * rows * columns,
    )(core.reshape(1), cotangent)


def head_kernel(
    factor,
    core_ref,
    kept_ref,
    theirs_ref,
    high_ref,
    coeffs_ref,
    out_ref,
    bias_ref,
    delta_ref,
    coef_ref,
    basis_ref,
    flipped,
    column,
    mine,
    other,
):
    step = pl.program_id(0)
    scans = kept_ref.shape[0]
    basis = basis_ref.shape[0]

    @pl.when(step == 0)
    def _():
        flipped[...] = out_ref[...].T
        column[...] = jnp.broadcast_to(bias_ref[...], (128, basis)).T
        mine[...] = jnp.zeros_like(mine)
        other[...] = jnp.zeros_like(other)

    for at in range(0, basis, CHUNK):
        rows = slice(at, at + CHUNK)
        summed = dot(flipped[rows, :], high_ref[...], ((1,), (0,))) + column[rows, :1]
        basis_ref[rows, :] = jnp.tanh(summed).astype(BF)
    for at in range(0, basis, CHUNK):
        rows = slice(at, at + CHUNK)
        mine[:, rows] += dot(kept_ref[...], basis_ref[rows, :], ((1,), (1,)))
        other[:, rows] += dot(theirs_ref[...], basis_ref[rows, :], ((1,), (1,)))
        pulled = dot(coeffs_ref[rows, :scans], kept_ref[...], ((1,), (0,)))
        pulled += dot(coeffs_ref[rows, scans:], theirs_ref[...], ((1,), (0,)))
        delta_ref[rows, :] = (factor * pulled * slope(basis_ref[rows, :])).astype(BF)

    @pl.when(step == pl.num_programs(0) - 1)
    def _():
        core = core_ref[0]
        coef_ref[pl.ds(pl.multiple_of(core * scans, scans), scans), :] = mine[...].astype(BF)
        coef_ref[pl.ds(pl.multiple_of((1 - core) * scans, scans), scans), :] = other[...].astype(BF)


def trunk_head(core, cotangent, theirs, high, coeffs, out, bias, factor):
    width, half = high.shape
    basis = out.shape[1]
    scans = cotangent.shape[0]
    steps = half // TILE
    return call(
        functools.partial(head_kernel, factor),
        steps,
        [
            pl.BlockSpec((scans, TILE), lambda i, c: (0, c[0] * steps + i)),
            pl.BlockSpec((scans, TILE), lambda i, c: (0, i)),
            pl.BlockSpec((width, TILE), lambda i, c: (0, i)),
            pl.BlockSpec((basis, 2 * scans), lambda i, c: (0, 0)),
            pl.BlockSpec((width, basis), lambda i, c: (0, 0)),
            pl.BlockSpec((1, basis), lambda i, c: (0, 0)),
        ],
        [
            pl.BlockSpec((basis, TILE), lambda i, c: (0, i)),
            pl.BlockSpec((2 * scans, basis), lambda i, c: (0, 0)),
        ],
        [
            jax.ShapeDtypeStruct((basis, half), BF),
            jax.ShapeDtypeStruct((2 * scans, basis), BF),
        ],
        [
            pltpu.VMEM((basis, TILE), BF),
            pltpu.VMEM((basis, width), BF),
            pltpu.VMEM((basis, 128), F32),
            pltpu.VMEM((scans, basis), F32),
            pltpu.VMEM((scans, basis), F32),
        ],
        2 * half * basis * (width + 4 * scans),
        15 * 1024 * 1024,
    )(core.reshape(1), cotangent, theirs, high, coeffs, out, bias.reshape(1, basis))


def load_kernel(factor, core_ref, parts_ref, mine_ref, swapped_ref, load_ref, coef):
    columns = mine_ref.shape[1]
    basis = parts_ref.shape[1]

    @pl.when(pl.program_id(0) == 0)
    def _():
        total = jnp.zeros((16, basis), F32)
        for at in range(0, parts_ref.shape[0], 16):
            total += parts_ref[at : at + 16, :].astype(F32)
        total = total * factor
        flat = jnp.concatenate([total[:8], total[8:]], axis=1)
        coef[...] = jnp.concatenate([flat, flat], axis=0).astype(BF)

    load_ref[:, :columns] = (mine_ref[...].astype(F32) + swapped_ref[...].astype(F32)).astype(BF)
    for at in range(0, load_ref.shape[0], 16):
        load_ref[at : at + 16, columns:] = coef[...]


def pack_load(core, parts, mine, swapped, factor):
    rows, columns = mine.shape
    basis = parts.shape[1]
    tile = 256
    return call(
        functools.partial(load_kernel, factor),
        rows // tile,
        [
            pl.BlockSpec(parts.shape, lambda i, c: (0, 0)),
            pl.BlockSpec((tile, columns), lambda i, c: (i, 0)),
            pl.BlockSpec((tile, columns), lambda i, c: (i, 0)),
        ],
        pl.BlockSpec((tile, columns + 2 * basis), lambda i, c: (i, 0)),
        jax.ShapeDtypeStruct((rows, columns + 2 * basis), BF),
        [pltpu.VMEM((16, 2 * basis), BF)],
        0,
        9 * 1024 * 1024,
    )(core.reshape(1), parts, mine, swapped)


def total_kernel(core_ref, got_ref, wide_ref, coef_ref):
    rows, columns = wide_ref.shape
    total = jnp.zeros((16, columns), F32)
    for at in range(0, rows, 16):
        total += got_ref[at : at + 16, :columns].astype(F32)
        coef_ref[at : at + 16, :] = got_ref[at : at + 16, columns:]
    total = total[:8] + total[8:]
    both = jnp.concatenate([total, total], axis=0).astype(BF)
    for at in range(0, rows, 16):
        wide_ref[at : at + 16, :] = both


def sum_spread(core, got, columns):
    rows, wide = got.shape
    return call(
        total_kernel,
        1,
        [pl.BlockSpec((rows, wide), lambda i, c: (0, 0))],
        [
            pl.BlockSpec((rows, columns), lambda i, c: (0, 0)),
            pl.BlockSpec((rows, wide - columns), lambda i, c: (0, 0)),
        ],
        [
            jax.ShapeDtypeStruct((rows, columns), BF),
            jax.ShapeDtypeStruct((rows, wide - columns), BF),
        ],
        [],
        0,
        2 * rows * wide * 2,
    )(core.reshape(1), got)


def unpack_kernel(core_ref, own_ref, *refs):
    mid_ref, out_ref, in_ref, zero_ref, one_ref, two_ref = refs[-6:]
    width, basis = mid_ref.shape[1], out_ref.shape[1]
    mid_ref[...] = own_ref[:, :width].astype(F32)
    out_ref[...] = own_ref[:, width : width + basis].astype(F32)
    small = own_ref[:, width + basis :].astype(F32).T
    in_ref[...] = small[:4]
    zero_ref[...] = small[4:5]
    one_ref[...] = small[5:6]
    kept = refs[5][...] if len(refs) > 6 else small[6:7]
    two_ref[...] = jnp.where(core_ref[0] == 0, small[6:7], kept)


def unpack(side, own, width, basis, earlier=()):
    rows, columns = own.shape
    tile = 256
    steps = rows // tile

    def row(i, c):
        return (c[0] * steps + i, 0)

    def lane(i, c):
        return (0, c[0] * steps + i)

    return pl.pallas_call(
        unpack_kernel,
        grid_spec=pltpu.PrefetchScalarGridSpec(
            num_scalar_prefetch=1,
            grid=(steps,),
            in_specs=[pl.BlockSpec((tile, columns), lambda i, c: (i, 0))]
            + [pl.BlockSpec(memory_space=pl.ANY)] * (len(earlier) - 1)
            + [pl.BlockSpec((1, tile), lambda i, c: (0, i))] * (len(earlier) > 0),
            out_specs=[
                pl.BlockSpec((tile, width), row),
                pl.BlockSpec((tile, basis), row),
                pl.BlockSpec((4, tile), lane),
                pl.BlockSpec((1, tile), lane),
                pl.BlockSpec((1, tile), lane),
                pl.BlockSpec((1, tile), lambda i, c: (0, i)),
            ],
        ),
        out_shape=[
            jax.ShapeDtypeStruct((width, width), F32),
            jax.ShapeDtypeStruct((width, basis), F32),
            jax.ShapeDtypeStruct((4, width), F32),
            jax.ShapeDtypeStruct((1, width), F32),
            jax.ShapeDtypeStruct((1, width), F32),
            jax.ShapeDtypeStruct((1, basis), F32),
        ],
        input_output_aliases={2 + at: at for at in range(len(earlier))},
        compiler_params=pltpu.CompilerParams(
            dimension_semantics=("arbitrary",), vmem_limit_bytes=16 * 1024 * 1024
        ),
        cost_estimate=pl.CostEstimate(
            flops=0, bytes_accessed=5 * 1024 * 1024, transcendentals=0
        ),
    )(side.reshape(1), own, *earlier)


def on_device(
    cotangent,
    scan_paths,
    query_points,
    branch_in,
    branch_in_bias,
    branch_out,
    branch_out_bias,
    trunk_in,
    trunk_in_bias,
    trunk_mid,
    trunk_mid_bias,
    trunk_out,
    trunk_out_bias,
):
    core = lax.axis_index("core")
    scan_rows, point_cols = cotangent.shape
    half = point_cols // 2
    chips = lax.axis_size(CHIPS)
    pts = lax.axis_size(PTS)
    factor = 1.0 / math.sqrt(scan_rows * 4 * point_cols * pts)
    width = trunk_in.shape[1]
    basis = trunk_out.shape[1]

    theirs = swap(take_other_half(core, cotangent), "core")
    pair_paths = swap(scan_paths, "core")
    zl = lax.axis_index("zl")
    points = lax.dynamic_slice_in_dim(query_points, core * half, half, 1)

    trunk_0 = dot(trunk_in, points, ((0,), (0,))) + trunk_in_bias[:, None]
    trunk_0 = jnp.tanh(trunk_0).astype(BF)
    trunk_1 = dot(trunk_mid[0], trunk_0, ((0,), (0,))) + trunk_mid_bias[0][:, None]
    trunk_1 = jnp.tanh(trunk_1).astype(BF)
    local_paths = jnp.concatenate([scan_paths, pair_paths], axis=0)
    side_paths = swap(local_paths, "zl")

    hidden_local = tanh_layer(local_paths, branch_in, branch_in_bias)
    coeffs = dot(branch_out, hidden_local, ((0,), (1,))) + branch_out_bias[:, None]
    coeffs = coeffs.astype(BF)

    delta_2, coef_part = trunk_head(
        core, cotangent, theirs, trunk_1, coeffs, trunk_out, trunk_out_bias, factor
    )
    coef_parts = exchange(coef_part, ("core",) + PTS)

    other, mine = trunk_back(
        core, delta_2, trunk_0, trunk_1, query_points, trunk_out, trunk_mid[0]
    )
    coef_parts, side_paths, other = lax.optimization_barrier((coef_parts, side_paths, other))

    columns = mine.shape[1]
    load = pack_load(core, coef_parts, mine, swap(other, "core"), factor)
    got = exchange(load, CHIPS)
    local = local_paths.reshape(2, scan_rows, -1)
    side = side_paths.reshape(2, scan_rows, -1)
    paths = jnp.where(
        zl == 0, jnp.stack([local, side], axis=1), jnp.stack([side, local], axis=1)
    ).reshape(4 * scan_rows, -1)
    hidden = tanh_layer(paths, branch_in, branch_in_bias)
    got, hidden = lax.optimization_barrier((got, hidden))
    wide, coef_own = sum_spread(core, got, columns)
    spread = exchange(wide, CHIPS)

    coef_all = jnp.stack([coef_own, swap(coef_own, "core")])
    rows = coef_own.shape[0] // chips
    coef_all = coef_all.reshape(2, chips, rows, 2, basis).transpose(0, 1, 3, 2, 4)
    coef_all = coef_all.reshape(4 * scan_rows, basis)
    grad_branch_out = rows_rows(hidden, coef_all)
    grad_branch_out_bias = dot(jnp.ones((8, 4 * scan_rows), BF), coef_all, ((1,), (0,)))[0]
    branch_delta = (dot(coef_all, branch_out, ((1,), (1,))) * slope(hidden)).astype(BF)
    grad_branch_in = rows_rows(paths, branch_delta)
    grad_branch_in_bias = jnp.sum(branch_delta.astype(F32), axis=0)

    spread, grad_branch_out, grad_branch_in, grad_branch_out_bias = lax.optimization_barrier(
        (spread, grad_branch_out, grad_branch_in, grad_branch_out_bias)
    )
    spread_theirs = swap(spread, "core")
    first = unpack(core, spread, width, basis)
    grad_mid, grad_out, grad_in, bias_0, bias_1, bias_2 = unpack(
        1 - core, spread_theirs, width, basis, first
    )
    return (
        grad_branch_in,
        grad_branch_in_bias,
        grad_branch_out,
        grad_branch_out_bias,
        grad_in,
        bias_0[0],
        grad_mid[None],
        bias_1,
        grad_out,
        bias_2[0],
    )


def solution(mesh):
    fine = Mesh(mesh.devices.reshape(2, 2, 4, 4, 2), ALL)
    scan, pts = ("zl", "core"), PTS
    placed = (P(scan, pts), P(scan, None), P(None, pts)) + (P(),) * 10
    return jax.shard_map(
        on_device, mesh=fine, in_specs=placed, out_specs=(P(),) * 10, check_vma=False
    )
```
